32 devices in a mesh: gx: 4 (over z), gy: 8 (over y, x, core).
Axes of the slice: x: 2, y: 2, z: 4, core: 2. Of those that a mesh axis runs over, the one named last changes fastest.
Arguments:
- velocity: float32 [3, 4, 128, 1024], P(None, 'gx', 'gy'), may hold values from -6 to 6
- y_metric: float32 [128], P('gy'), may hold values from 0.5 to 4
- forward_rate: float32 [3, 128], P(None, 'gy'), may hold values from 0.96875 to 1
- backward_rate: float32 [3, 128], P(None, 'gy'), may hold values from 0.96875 to 1
- pivot_inv: float32 [3, 128], P(None, 'gy'), may hold values from 0 to 0.01171875
- particle_vel: float32 [3, 114688], P(None, ('gx', 'gy')), may hold values from -6 to 6
- particle_cell: int32 [114688], P(('gx', 'gy')), may hold values from 0 to 16383
- particle_offset: float32 [3, 114688], P(None, ('gx', 'gy')), may hold values from 0 to 1
- inverse_tau: float32 [114688], P(('gx', 'gy')), may hold values from 0.5 to 8
- outgoing_count: int32 [4, 8, 3], P('gx', 'gy'), may hold values from 0 to 512, as said below
Outputs:
- velocity_out: float32 [3, 4, 128, 1024], P(None, 'gx', 'gy')
- particle_out: float32 [3, 114688], P(None, ('gx', 'gy'))
The draws below stay inside these ranges and needn't reach their ends.
Inputs may be any that keep to these rules, and one draw needn't show every extreme that they name: `outgoing_count`: entry d of a block counts the live leading slots of its outgoing block d; the -y block of the lowest and the +y block of the highest wall-normal blocks are empty; some +x block is full.
All inputs are finite; a program needn't handle non-finite values.
Results may differ from the reference program's by a relative error of at most 0.00029.
Values sent between devices are 32-bit elements; how exact they have to be, the bound alone decides.
No kernel may reach another device: no remote copies, remote signals or barrier semaphores. Data moves between devices by JAX's collectives and lax.ppermute only.
A program may use at most 192 MiB of HBM per device.

```python
import math
import jax
import jax.numpy as jnp
from jax import lax

CX = 1
CY = 16
CZ = 1024
RESIDENT = 2048
CAP = 512
SECTIONS = 3
NX = 4
NY = 128
NZ = 1024
CELLS = 16384
SLOTS = 3584
PARTS_SIZE = 114688
N_GX = 4
N_GY = 8


def rate_triple(key):
    first = jax.random.uniform(jax.random.fold_in(key, 11), (SECTIONS, NY), jnp.float32)
    second = jax.random.uniform(jax.random.fold_in(key, 12), (SECTIONS, NY), jnp.float32)
    third = jax.random.uniform(jax.random.fold_in(key, 13), (SECTIONS, NY), jnp.float32)
    down_strength = 0.25 * jnp.exp(jnp.log(16.0) * first)
    up_strength = 0.25 * jnp.exp(jnp.log(16.0) * second)
    gain = 3.0 * jnp.exp(jnp.log(4.0) * third)
    down_rate = jnp.exp(-down_strength / NY)
    up_rate = jnp.exp(-up_strength / NY)
    scale_rate = (1.0 - down_rate) * (1.0 - up_rate) * gain
    return (down_rate, up_rate, scale_rate)


def draw_forward_rate(key, part):
    return rate_triple(key)[0]


def draw_backward_rate(key, part):
    return rate_triple(key)[1]


def draw_pivot_inv(key, part):
    return rate_triple(key)[2]


def draw_outgoing_count(key, part):
    counts = jax.random.randint(jax.random.fold_in(key, 21), (N_GX, N_GY, 3), 0, CAP + 1)
    place_x = jax.random.randint(jax.random.fold_in(key, 22), (), 0, N_GX)
    place_y = jax.random.randint(jax.random.fold_in(key, 23), (), 0, N_GY)
    counts = counts.at[:, 0, 1].set(0)
    counts = counts.at[:, N_GY - 1, 2].set(0)
    counts = counts.at[place_x, place_y, 0].set(CAP)
    return counts.astype(jnp.int32)


def plant(drawn, key, low, top_value):
    index_at = [jax.random.randint(jax.random.fold_in(key, axis), (), 0, length) for axis, length in enumerate(drawn.shape)]
    main_axis = drawn.shape.index(max(drawn.shape))
    neighbour = index_at[:main_axis] + [(index_at[main_axis] + 1) % drawn.shape[main_axis]] + index_at[main_axis + 1:]
    return drawn.at[tuple(index_at)].set(low).at[tuple(neighbour)].set(top_value)


def levels(own_key, shape, pieces, low, largest):
    def one(axis_at, parts):
        heights = jax.random.uniform(jax.random.fold_in(jax.random.fold_in(own_key, 6), axis_at), (parts,), jnp.float32, low / len(pieces), largest / len(pieces))
        return jnp.repeat(jnp.exp(heights), shape[axis_at] // parts).reshape((-1,) + (1,) * (len(shape) - axis_at - 1))

    level = one(*pieces[0])
    for cut in pieces[1:]:
        level = level * one(*cut)
    return level


def scatter_about(stream_key, dims, deviation, reach, split=(), held_as=jnp.bfloat16):
    entries = jax.random.normal(stream_key, dims, jnp.float32) * deviation
    if len(split) > 0:
        entries = levels(stream_key, dims, split, -0.22, 0.18) * entries
    return jnp.clip(entries, min=-reach, max=reach).astype(held_as)


def setup_inputs(seed: int = 0) -> dict:
    splits = jax.random.split(jax.random.key(seed), 11)
    velocity = scatter_about(splits[0], (3, NX, NY, NZ), 1.0, 6.0, ((1, 4), (2, 8)), jnp.float32)
    y_metric = jnp.clip(jnp.exp(math.log(4.0) - 2.0794415 * jax.random.uniform(splits[1], (NY,), jnp.float32) ** levels(splits[1], (NY,), ((0, 8),), -0.2, 0.2)), 0.5, 4.0)
    forward_rate = draw_forward_rate(jax.random.fold_in(splits[10], 71), 0)
    backward_rate = draw_backward_rate(jax.random.fold_in(splits[10], 71), 0)
    pivot_inv = draw_pivot_inv(jax.random.fold_in(splits[10], 71), 0)
    particle_vel = scatter_about(splits[5], (3, PARTS_SIZE), 1.0, 6.0, ((1, 32),), jnp.float32)
    particle_cell = plant(jax.random.randint(splits[6], (PARTS_SIZE,), 0, CELLS), jax.random.fold_in(splits[6], 1), 0, CELLS - 1).astype(jnp.int32)
    particle_offset = jnp.clip(1.0 * jax.random.uniform(splits[7], (3, PARTS_SIZE), jnp.float32) ** levels(splits[7], (3, PARTS_SIZE), ((1, 32),), -0.2, 0.2), 0.0, 1.0)
    inverse_tau = jnp.clip(jnp.exp(math.log(8.0) - 2.7725887 * jax.random.uniform(splits[8], (PARTS_SIZE,), jnp.float32) ** levels(splits[8], (PARTS_SIZE,), ((0, 32),), -0.2, 0.2)), 0.5, 8.0)
    outgoing_count = draw_outgoing_count(jax.random.fold_in(splits[10], 71), 0)
    return {"velocity": velocity, "y_metric": y_metric, "forward_rate": forward_rate, "backward_rate": backward_rate, "pivot_inv": pivot_inv, "particle_vel": particle_vel, "particle_cell": particle_cell, "particle_offset": particle_offset, "inverse_tau": inverse_tau, "outgoing_count": outgoing_count}


SECTION_WEIGHTS = (8.0 / 15.0, 5.0 / 12.0, 3.0 / 4.0)
TIME_STEP = 0.3
STREAM_SCALE = 2.0
SPAN_SCALE = 2.0
COUPLING = 0.5
CORNER_LIST = ((0, 0, 0), (0, 0, 1), (0, 1, 0), (0, 1, 1), (1, 0, 0), (1, 0, 1), (1, 1, 0), (1, 1, 1))


def stencil(field, upper_x, lower_x, upper_y, lower_y, upper_z, lower_z, y_metric):
    slope_x = (upper_x - lower_x) * (0.5 * STREAM_SCALE)
    slope_y = (upper_y - lower_y) * (0.5 * y_metric)[None, None, :, None]
    slope_z = (upper_z - lower_z) * (0.5 * SPAN_SCALE)
    return -(field[0:1] * slope_x + field[1:2] * slope_y + field[2:3] * slope_z)


def corner_weight(offsets, corner):
    weight = None
    for dimension in range(3):
        factor = offsets[dimension] if corner[dimension] else 1.0 - offsets[dimension]
        weight = factor if weight is None else weight * factor
    return weight


def convect(field, y_metric):
    padded = jnp.pad(field, ((0, 0), (0, 0), (1, 1), (0, 0)))
    return stencil(field, jnp.roll(field, -1, axis=1), jnp.roll(field, 1, axis=1),
                   padded[:, :, 2:, :], padded[:, :, :-2, :],
                   jnp.roll(field, -1, axis=3), jnp.roll(field, 1, axis=3), y_metric)


def solve(rhs, down_rate, up_rate, scale_rate):
    rows = jnp.moveaxis(rhs, 2, 0)

    def downward(carry, item):
        value, rate = item
        result = value + rate * carry
        return result, result

    def upward(carry, item):
        value, rate, scale = item
        result = scale * value + rate * carry
        return result, result

    start = jnp.zeros_like(rows[0])
    _, forward = lax.scan(downward, start, (rows, down_rate))
    _, backward = lax.scan(upward, start, (forward, up_rate, scale_rate), reverse=True)
    return jnp.moveaxis(backward, 0, 2)


def reference(velocity, y_metric, forward_rate, backward_rate, pivot_inv, particle_vel, particle_cell, particle_offset, inverse_tau, outgoing_count):
    position = jnp.arange(PARTS_SIZE, dtype=jnp.int32)
    slot_num = position % SLOTS
    block = position // SLOTS
    block_x = block // N_GY
    block_y = block % N_GY
    remain = slot_num - RESIDENT
    heading = jnp.clip(remain // CAP, 0, 2)
    limit = outgoing_count[block_x, block_y, heading]
    live = jnp.where((slot_num < RESIDENT) | (remain % CAP < limit), 1.0, 0.0).astype(jnp.float32)
    cell_x = particle_cell // (CY * CZ)
    cell_y = (particle_cell // CZ) % CY
    cell_z = particle_cell % CZ
    global_x = block_x * CX + cell_x
    global_y = block_y * CY + cell_y
    flat_cell = (global_x * NY + global_y) * NZ + cell_z
    field = velocity
    moving = particle_vel
    for section_num in range(SECTIONS):
        step_size = TIME_STEP * SECTION_WEIGHTS[section_num]
        extended = jnp.concatenate([field, field[:, :1]], axis=1)
        extended = jnp.pad(extended, ((0, 0), (0, 0), (0, 1), (0, 0)))
        fluid_at = jnp.zeros_like(moving)
        for corner in CORNER_LIST:
            values = extended[:, global_x + corner[0], global_y + corner[1], (cell_z + corner[2]) % NZ]
            fluid_at = fluid_at + corner_weight(particle_offset, corner) * values
        drag = inverse_tau * (fluid_at - moving)
        moving = moving + step_size * drag
        force = jnp.zeros((3, NX * NY * NZ), jnp.float32).at[:, flat_cell].add(-COUPLING * drag * live)
        rhs = field + step_size * (convect(field, y_metric) + force.reshape(field.shape))
        field = solve(rhs, forward_rate[section_num], backward_rate[section_num], pivot_inv[section_num])
    masked = moving * live
    grid = masked.reshape(3, N_GX, N_GY, SLOTS)
    kept = grid[..., :RESIDENT]
    to_x = grid[..., RESIDENT:RESIDENT + CAP]
    to_lower = grid[..., RESIDENT + CAP:RESIDENT + 2 * CAP]
    to_upper = grid[..., RESIDENT + 2 * CAP:]
    from_x = jnp.roll(to_x, 1, axis=1)
    empty = jnp.zeros_like(to_x[:, :, :1])
    from_above = jnp.concatenate([to_lower[:, :, 1:], empty], axis=2)
    from_below = jnp.concatenate([empty, to_upper[:, :, :-1]], axis=2)
    moved = jnp.concatenate([kept, from_x, from_above, from_below], axis=3).reshape(3, PARTS_SIZE)
    return field, moved
```

```python
import functools

import jax
import jax.numpy as jnp
from jax import lax
from jax.experimental import pallas as pl
from jax.experimental.pallas import tpu as pltpu
from jax.sharding import PartitionSpec as P

RESIDENT = 2048
CAP = 512
SECTIONS = 3

SECTION_WEIGHTS = (8.0 / 15.0, 5.0 / 12.0, 3.0 / 4.0)
TIME_STEP = 0.3
STREAM_SCALE = 2.0
SPAN_SCALE = 2.0
COUPLING = 0.5
COMPS = 3
TILE = 512
DEPTH = 256
VMEM_LIMIT = 24 * 1024 * 1024

F32 = jnp.float32
BF16 = jnp.bfloat16


def params():
    return pltpu.CompilerParams(vmem_limit_bytes=VMEM_LIMIT)


def whole_in_vmem(count):
    return [pl.BlockSpec(memory_space=pltpu.VMEM)] * count


def selector(column, depth_total):
    width = column.shape[1]
    shape = (DEPTH // 16, 16, width)
    order = lax.broadcasted_iota(jnp.int32, shape, 0) * 16 + lax.broadcasted_iota(jnp.int32, shape, 1)
    order = order.astype(F32).astype(BF16)
    one, none = jnp.ones((), BF16), jnp.zeros((), BF16)
    tiles = []
    for k in range(depth_total // DEPTH):
        wanted = jnp.broadcast_to(column - float(DEPTH * k), (16, width)).astype(BF16)
        tiles.append(jnp.where(order == wanted[None], one, none).reshape(DEPTH, width))
    return tiles


def split_rows(rows):
    length = rows.shape[1]
    high = rows.astype(BF16).astype(F32)
    low = rows - high
    ahead = [pltpu.roll(part, length - 1, 1) for part in (high, low)]
    return jnp.concatenate([high, low] + ahead, axis=0).astype(BF16)


def looked_up(table_ref, tiles):
    total = None
    for k, tile in enumerate(tiles):
        part = jnp.dot(
            table_ref[:, DEPTH * k : DEPTH * (k + 1)], tile, preferred_element_type=F32
        )
        total = part if total is None else total + part
    return total


def blend_z(values, fz):
    rows = values.shape[0] // 4
    near = values[:rows] + values[rows : 2 * rows]
    far = values[2 * rows : 3 * rows] + values[3 * rows :]
    return near * (1.0 - fz) + far * fz


def own_plane_kernel(cells_z, u_ref, cell_ref, off_ref, out_ref, table_ref):
    rows = u_ref.shape[0] // COMPS
    table_ref[...] = split_rows(u_ref[...])

    @pl.loop(0, cell_ref.shape[1] // TILE)
    def _(t):
        here = pl.ds(pl.multiple_of(t * TILE, TILE), TILE)
        cell = cell_ref[:, here]
        row, column = cell // cells_z, (cell % cells_z).astype(F32)
        fx, fy, fz = (off_ref[d : d + 1, here] for d in range(3))
        blended = blend_z(looked_up(table_ref, selector(column, cells_z)), fz)
        order = lax.broadcasted_iota(jnp.int32, (rows, TILE), 0)
        weight = jnp.where(order == row, 1.0 - fy, jnp.where(order == row + 1, fy, 0.0))
        weight = weight * (1.0 - fx)
        for c in range(COMPS):
            part = blended[rows * c : rows * (c + 1)] * weight
            out_ref[c : c + 1, here] = jnp.sum(part, axis=0, keepdims=True)


def section_kernel(
    cells_z,
    step,
    last,
    info_ref,
    u_ref,
    xp_ref,
    xm_ref,
    yp_ref,
    ym_ref,
    corner_ref,
    cell_ref,
    off_ref,
    tau_ref,
    v_ref,
    near_ref,
    metric_ref,
    mat_ref,
    scal_ref,
    w_ref,
    pq_ref,
    v_out_ref,
    table_ref,
    force_ref,
):
    rows = u_ref.shape[0] // COMPS
    top = jnp.where(info_ref[4] == 0, 0.0, 1.0).astype(F32)
    bottom = jnp.where(info_ref[3] == 0, 0.0, 1.0).astype(F32)
    y_plus = yp_ref[...] * top
    y_minus = ym_ref[...] * bottom
    corner = corner_ref[...] * top
    pad = jnp.zeros((2, cells_z), F32)
    table_ref[...] = split_rows(jnp.concatenate([xp_ref[...], y_plus, corner, pad], axis=0))
    force_ref[...] = jnp.zeros_like(force_ref)

    @pl.loop(0, cell_ref.shape[1] // TILE)
    def _(t):
        here = pl.ds(pl.multiple_of(t * TILE, TILE), TILE)
        cell = cell_ref[:, here]
        row, column = cell // cells_z, (cell % cells_z).astype(F32)
        fx, fy, fz = (off_ref[d : d + 1, here] for d in range(3))
        tiles = selector(column, cells_z)
        blended = blend_z(looked_up(table_ref, tiles), fz)
        order = lax.broadcasted_iota(jnp.int32, (rows, TILE), 0)
        at_row = order == row
        weight = jnp.where(at_row, 1.0 - fy, jnp.where(order == row + 1, fy, 0.0)) * fx
        edge = jnp.where(row == rows - 1, fy, 0.0)
        slot = t * TILE + lax.broadcasted_iota(jnp.int32, (1, TILE), 1)
        remain = slot - RESIDENT
        heading = remain // CAP
        limit = jnp.where(
            heading <= 0, info_ref[0], jnp.where(heading == 1, info_ref[1], info_ref[2])
        )
        live = jnp.where((remain < 0) | (remain % CAP < limit), 1.0, 0.0)
        base = COMPS * rows
        tau = tau_ref[:, here]
        spread = []
        for c in range(COMPS):
            part = jnp.sum(blended[rows * c : rows * (c + 1)] * weight, axis=0, keepdims=True)
            side = blended[base + c : base + c + 1] * (1.0 - fx)
            side = side + blended[base + COMPS + c : base + COMPS + c + 1] * fx
            fluid = near_ref[c : c + 1, here] + part + side * edge
            v = v_ref[c : c + 1, here]
            drag = tau * (fluid - v)
            v = v + step * drag
            v_out_ref[c : c + 1, here] = v * live if last else v
            spread.append(jnp.where(at_row, drag * live * (-COUPLING), 0.0))
        spread = jnp.concatenate(spread, axis=0)
        high = spread.astype(BF16).astype(F32)
        spread = jnp.concatenate([high, spread - high], axis=0).astype(BF16)
        for k, tile in enumerate(tiles):
            force_ref[:, DEPTH * k : DEPTH * (k + 1)] += lax.dot_general(
                spread, tile, (((1,), (1,)), ((), ())), preferred_element_type=F32
            )

    u = u_ref[...]
    slope_x = (xp_ref[...] - xm_ref[...]) * (0.5 * STREAM_SCALE)
    slope_z = (pltpu.roll(u, cells_z - 1, 1) - pltpu.roll(u, 1, 1)) * (0.5 * SPAN_SCALE)
    metric = 0.5 * metric_ref[...]
    count = COMPS * rows
    rhs = []
    for c in range(COMPS):
        own = slice(rows * c, rows * (c + 1))
        field = u[own]
        upper = jnp.concatenate([field[1:], y_plus[c : c + 1]], axis=0)
        lower = jnp.concatenate([y_minus[c : c + 1], field[:-1]], axis=0)
        slope_y = (upper - lower) * metric
        convection = -(
            u[:rows] * slope_x[own] + u[rows : 2 * rows] * slope_y + u[2 * rows :] * slope_z[own]
        )
        force = force_ref[own, :] + force_ref[count + rows * c : count + rows * (c + 1), :]
        rhs.append(field + step * (convection + force))
    solved = jnp.dot(
        mat_ref[...],
        jnp.concatenate(rhs, axis=0),
        precision=lax.Precision.HIGHEST,
        preferred_element_type=F32,
    )
    w_ref[...] = solved[:count]
    pq_ref[0:COMPS, :] = solved[count : count + COMPS]
    for c in range(COMPS):
        pq_ref[COMPS + c : COMPS + c + 1, :] = solved[rows * c : rows * c + 1]
    pq_ref[6:7, :] = scal_ref[...]
    pq_ref[7:8, :] = jnp.zeros_like(scal_ref)


def join_kernel(last, info_ref, all_ref, w_ref, enter_ref, leave_ref, u_ref, *more):
    blocks = all_ref.shape[0]
    rows = w_ref.shape[0] // COMPS
    here = info_ref[3]
    scal = [[all_ref[k, 6:7, i : i + 1] for i in range(5)] for k in range(blocks)]
    entering = jnp.zeros(all_ref.shape[1:], F32)[:COMPS]
    zero = entering
    at = []
    own_in = zero
    below = [jnp.zeros((1, 1), F32)] * 2
    for k in range(blocks):
        at.append(entering)
        own_in = jnp.where(here == k, entering, own_in)
        below = [jnp.where(here == k + 1, scal[k][3 + i], below[i]) for i in range(2)]
        entering = all_ref[k, 0:COMPS, :] + scal[k][0] * entering
    leaving = zero
    own_out = zero
    for k in reversed(range(blocks)):
        own_out = jnp.where(here == k, leaving, own_out)
        leaving = all_ref[k, COMPS : 2 * COMPS, :] + scal[k][2] * at[k] + scal[k][1] * leaving
    for c in range(COMPS):
        own = slice(rows * c, rows * (c + 1))
        u_ref[own, :] = (
            w_ref[own, :]
            + enter_ref[...] * own_in[c : c + 1]
            + leave_ref[...] * own_out[c : c + 1]
        )
    if not last:
        yp_ref, ym_ref = more
        yp_ref[...] = own_out
        for c in range(COMPS):
            ym_ref[c : c + 1, :] = (
                below[0] * own_in[c : c + 1] + below[1] * u_ref[rows * c : rows * c + 1, :]
            )


def block_tables(forward_rate, backward_rate, pivot_inv):
    rows = forward_rate.shape[1]
    i = jnp.arange(rows)[:, None, None]
    j = jnp.arange(rows + 1)[None, :, None]
    m = jnp.arange(rows)[None, None, :]
    lower = jnp.prod(
        jnp.where((m >= j) & (m <= i), forward_rate[:, None, None, :], 1.0), axis=-1
    ) * jnp.where(i >= j - 1, 1.0, 0.0)[..., 0]
    upper = jnp.prod(
        jnp.where((m >= i) & (m < j), backward_rate[:, None, None, :], 1.0), axis=-1
    ) * jnp.where(j >= i, 1.0, 0.0)[..., 0]
    both = jnp.sum(
        upper[:, :, :rows, None] * (pivot_inv[:, :, None] * lower)[:, None, :, :], axis=2
    )
    eye = jnp.eye(COMPS, dtype=F32)
    body = (eye[None, :, None, :, None] * both[:, None, :, None, 1:]).reshape(
        SECTIONS, COMPS * rows, COMPS * rows
    )
    tail = (eye[None, :, :, None] * lower[:, None, None, -1, 1:]).reshape(
        SECTIONS, COMPS, COMPS * rows
    )
    matrix = jnp.concatenate(
        [body, tail, jnp.zeros((SECTIONS, 8 - COMPS, COMPS * rows), F32)], axis=1
    )
    enter, leave = both[:, :, 0], upper[:, :, -1]
    scal = jnp.stack(
        [lower[:, -1, 0], leave[:, 0], enter[:, 0], pivot_inv[:, -1], backward_rate[:, -1]], axis=1
    )
    return matrix, enter[:, :, None], leave[:, :, None], scal


def on_device(
    velocity,
    y_metric,
    forward_rate,
    backward_rate,
    pivot_inv,
    particle_vel,
    particle_cell,
    particle_offset,
    inverse_tau,
    outgoing_count,
):
    comps, cells_x, cells_y, cells_z = velocity.shape
    assert (comps, cells_x) == (COMPS, 1)
    slots = particle_vel.shape[1]
    size_x, size_y = lax.axis_size("gx"), lax.axis_size("gy")
    ring_x = [(i, (i + 1) % size_x) for i in range(size_x)]
    back_x = [(b, a) for a, b in ring_x]
    ring_y = [(i, (i + 1) % size_y) for i in range(size_y)]
    back_y = [(b, a) for a, b in ring_y]
    diagonal = [
        (((x + 1) % size_x) * size_y + (y + 1) % size_y, x * size_y + y)
        for x in range(size_x)
        for y in range(size_y)
    ]
    position = lax.axis_index("gy")
    info = jnp.concatenate(
        [
            outgoing_count.reshape(3),
            jnp.stack([position, size_y - 1 - position]).astype(jnp.int32),
        ]
    )
    u = velocity.reshape(COMPS * cells_y, cells_z)
    first = velocity[:, 0, 0, :]
    final = velocity[:, 0, cells_y - 1, :]
    xp = lax.ppermute(u, "gx", back_x)
    xm = lax.ppermute(u, "gx", ring_x)
    yp = lax.ppermute(first, "gy", back_y)
    ym = lax.ppermute(final, "gy", ring_y)
    corner = lax.ppermute(first, ("gx", "gy"), diagonal)

    cell = particle_cell.reshape(1, slots)
    tau = inverse_tau.reshape(1, slots)
    metric = y_metric.reshape(cells_y, 1)
    matrix, enter, leave, scal = block_tables(forward_rate, backward_rate, pivot_inv)
    scal = jnp.pad(scal, ((0, 0), (0, cells_z - scal.shape[1])))
    v = particle_vel
    field_like = jax.ShapeDtypeStruct(u.shape, F32)
    edge_like = jax.ShapeDtypeStruct((COMPS, cells_z), F32)
    slots_like = jax.ShapeDtypeStruct((COMPS, slots), F32)
    smem = pl.BlockSpec(memory_space=pltpu.SMEM)
    for k in range(SECTIONS):
        last = k == SECTIONS - 1
        near = pl.pallas_call(
            functools.partial(own_plane_kernel, cells_z),
            out_shape=slots_like,
            in_specs=whole_in_vmem(3),
            out_specs=whole_in_vmem(1)[0],
            scratch_shapes=[pltpu.VMEM((4 * u.shape[0], cells_z), BF16)],
            compiler_params=params(),
            cost_estimate=pl.CostEstimate(
                flops=8 * u.shape[0] * cells_z * slots, bytes_accessed=1 << 18, transcendentals=0
            ),
            name="own_plane",
        )(u, cell, particle_offset)
        w, pq, v = pl.pallas_call(
            functools.partial(
                section_kernel, cells_z, TIME_STEP * SECTION_WEIGHTS[k], last
            ),
            out_shape=(field_like, jax.ShapeDtypeStruct((8, cells_z), F32), slots_like),
            in_specs=[smem] + whole_in_vmem(14),
            out_specs=tuple(whole_in_vmem(3)),
            scratch_shapes=[
                pltpu.VMEM((4 * (u.shape[0] + 8), cells_z), BF16),
                pltpu.VMEM((2 * u.shape[0], cells_z), F32),
            ],
            compiler_params=params(),
            name="section",
        )(
            info, u, xp, xm, yp, ym, corner, cell, particle_offset, tau, v, near, metric,
            matrix[k], scal[k : k + 1],
        )
        if last:
            from_x = lax.ppermute(v[:, RESIDENT : RESIDENT + CAP], "gx", ring_x)
            from_above = lax.ppermute(v[:, RESIDENT + CAP : RESIDENT + 2 * CAP], "gy", back_y)
            from_below = lax.ppermute(v[:, RESIDENT + 2 * CAP :], "gy", ring_y)
        gathered = lax.all_gather(pq, "gy", axis=0)
        joined = pl.pallas_call(
            functools.partial(join_kernel, last),
            out_shape=(field_like,) + (() if last else (edge_like, edge_like)),
            in_specs=[smem] + whole_in_vmem(4),
            out_specs=tuple(whole_in_vmem(1 if last else 3)),
            compiler_params=params(),
            name="join",
        )(info, gathered, w, enter[k], leave[k])
        u = joined[0]
        if not last:
            yp, ym = joined[1:]
            xp = lax.ppermute(u, "gx", back_x)
            xm = lax.ppermute(u, "gx", ring_x)
            corner = lax.ppermute(yp, "gx", back_x)
    moved = jnp.concatenate([v[:, :RESIDENT], from_x, from_above, from_below], axis=1)
    return (u.reshape(velocity.shape), moved)


def solution(mesh):
    return jax.shard_map(
        on_device,
        mesh=mesh,
        in_specs=(
            P(None, "gx", "gy", None),
            P("gy"),
            P(None, "gy"),
            P(None, "gy"),
            P(None, "gy"),
            P(None, ("gx", "gy")),
            P(("gx", "gy")),
            P(None, ("gx", "gy")),
            P(("gx", "gy")),
            P("gx", "gy", None),
        ),
        out_specs=(P(None, "gx", "gy", None), P(None, ("gx", "gy"))),
        check_vma=False,
    )
```

```python
import functools

import jax
import jax.numpy as jnp
from jax import lax
from jax.experimental import pallas as pl
from jax.experimental.pallas import tpu as pltpu
from jax.sharding import PartitionSpec as P

RESIDENT = 2048
CAP = 512
SECTIONS = 3

SECTION_WEIGHTS = (8.0 / 15.0, 5.0 / 12.0, 3.0 / 4.0)
TIME_STEP = 0.3
STREAM_SCALE = 2.0
SPAN_SCALE = 2.0
COUPLING = 0.5
COMPS = 3
TILE = 512
DEPTH = 256
VMEM_LIMIT = 32 * 1024 * 1024
ENTER, LEAVE, PIVOT, UPWARD, METRIC = range(16, 21)

F32 = jnp.float32
BF16 = jnp.bfloat16


def call(kernel, out_shape, in_specs, name, scratch_shapes=()):
    several = isinstance(out_shape, tuple)
    out_specs = whole_in_vmem(len(out_shape)) if several else whole_in_vmem(1)[0]
    return pl.pallas_call(
        kernel,
        out_shape=out_shape,
        in_specs=in_specs,
        out_specs=tuple(out_specs) if several else out_specs,
        scratch_shapes=scratch_shapes,
        compiler_params=pltpu.CompilerParams(vmem_limit_bytes=VMEM_LIMIT),
        name=name,
    )


def whole_in_vmem(count):
    return [pl.BlockSpec(memory_space=pltpu.VMEM)] * count


def scalars(count):
    return [pl.BlockSpec(memory_space=pltpu.SMEM)] * count


def across(row, depth):
    width = row.shape[1]
    shape = (DEPTH // 16, 16, width)
    order = lax.broadcasted_iota(jnp.int32, shape, 0) * 16 + lax.broadcasted_iota(jnp.int32, shape, 1)
    order = order.astype(F32).astype(BF16)
    one, none = jnp.ones((), BF16), jnp.zeros((), BF16)
    parts = []
    for k in range(depth // DEPTH):
        wanted = jnp.broadcast_to(row - float(DEPTH * k), (16, width)).astype(BF16)
        parts.append(jnp.where(order == wanted[None], one, none).reshape(DEPTH, width))
    return jnp.concatenate(parts, axis=0)


def down(row, depth):
    width = row.shape[1]
    order = lax.broadcasted_iota(jnp.int32, (width, DEPTH), 1).astype(F32).astype(BF16)
    one, none = jnp.ones((), BF16), jnp.zeros((), BF16)
    column = jnp.broadcast_to(row, (8, width)).T[:, 0:1]
    parts = []
    for k in range(depth // DEPTH):
        wanted = jnp.broadcast_to(column - float(DEPTH * k), (width, DEPTH)).astype(BF16)
        parts.append(jnp.where(order == wanted, one, none))
    return jnp.concatenate(parts, axis=1)


def split_rows(rows):
    length = rows.shape[1]
    high = rows.astype(BF16).astype(F32)
    low = rows - high
    ahead = [pltpu.roll(part, length - 1, 1) for part in (high, low)]
    return jnp.concatenate([high, low] + ahead, axis=0).astype(BF16)


def blend_z(values, fz):
    rows = values.shape[0] // 4
    near = values[:rows] + values[rows : 2 * rows]
    far = values[2 * rows : 3 * rows] + values[3 * rows :]
    return near * (1.0 - fz) + far * fz


def tables_kernel(down_ref, up_ref, scale_ref, metric_ref, matrix_ref, answer_ref, scal_ref):
    sections, rows = down_ref.shape
    lane = lax.broadcasted_iota(jnp.int32, (1, 128), 1)
    at = lambda place: jnp.where(lane == place, 1.0, 0.0)
    matrix_ref[...] = jnp.zeros_like(matrix_ref)
    scal_ref[...] = jnp.zeros_like(scal_ref)
    for k in range(sections):
        lower = []
        row = at(ENTER)
        for i in range(rows):
            row = down_ref[k, i] * row + at(i)
            lower.append(row)
        last = jnp.where(lane < rows, row, 0.0)
        for c in range(COMPS):
            place = COMPS * rows + c
            matrix_ref[k, place : place + 1, :] = pltpu.roll(last, rows * c, 1)
        scal_ref[k, 0:1, :] = row
        row = at(LEAVE)
        for i in reversed(range(rows)):
            row = scale_ref[k, i] * lower[i] + up_ref[k, i] * row
            inner = jnp.where(lane < rows, row, 0.0)
            for c in range(COMPS):
                place = rows * c + i
                matrix_ref[k, place : place + 1, :] = inner if c == 0 else pltpu.roll(inner, rows * c, 1)
            answer_ref[k, i : i + 1, :] = row + metric_ref[i] * at(METRIC)
        scal_ref[k, 1:2, :] = (
            row + scale_ref[k, rows - 1] * at(PIVOT) + up_ref[k, rows - 1] * at(UPWARD)
        )


def own_plane_kernel(u_ref, cell_ref, off_ref, out_ref, table_ref):
    cells_z = u_ref.shape[1]
    rows = u_ref.shape[0] // COMPS
    table_ref[...] = split_rows(u_ref[...])
    order = lax.broadcasted_iota(jnp.int32, (rows, TILE), 0)
    for t in range(cell_ref.shape[1] // TILE):
        here = slice(t * TILE, (t + 1) * TILE)
        cell = cell_ref[:, here]
        row = cell // cells_z
        fx, fy, fz = (off_ref[d : d + 1, here] for d in range(3))
        chosen = across((cell % cells_z).astype(F32), cells_z)
        blended = blend_z(jnp.dot(table_ref[...], chosen, preferred_element_type=F32), fz)
        weight = jnp.where(order == row, 1.0 - fy, jnp.where(order == row + 1, fy, 0.0))
        weight = weight * (1.0 - fx)
        for c in range(COMPS):
            part = blended[rows * c : rows * (c + 1)] * weight
            out_ref[c : c + 1, here] = jnp.sum(part, axis=0, keepdims=True)


def section_kernel(number, step, last, *refs):
    first = number == 0
    refs = list(refs)
    take = lambda count: [refs.pop(0) for _ in range(count)]
    count_ref, u_ref, ym_ref, xp_ref, xm_ref, yp_ref, ahead_ref = take(7)
    behind_ref = None if first else refs.pop(0)
    cell_ref, off_ref, tau_ref, v_ref, near_ref, matrix_ref, answer_ref, scal_ref = take(8)
    w_ref, pq_ref, v_out_ref = take(3)
    leaving_ref = refs.pop(0) if last else None
    table_ref, spread_ref, chosen_ref = refs

    cells_z = u_ref.shape[1]
    rows = u_ref.shape[0] // COMPS
    count = COMPS * rows
    position = lax.axis_index("gy")
    top = jnp.where(position == lax.axis_size("gy") - 1, 0.0, 1.0).astype(F32)
    bottom = jnp.where(position == 0, 0.0, 1.0).astype(F32)
    y_minus = ym_ref[...] * bottom
    x_plus, x_minus = xp_ref[...], xm_ref[...]
    if first:
        y_plus = yp_ref[...] * top
        corner = ahead_ref[...] * top
    else:
        y_plus = yp_ref[COMPS : 2 * COMPS, :]
        corner = ahead_ref[COMPS : 2 * COMPS, :]
        enter = answer_ref[number - 1, :, ENTER : ENTER + 1]
        leave = answer_ref[number - 1, :, LEAVE : LEAVE + 1]

        def joined(plane, ref):
            return jnp.concatenate(
                [
                    plane[rows * c : rows * (c + 1)]
                    + enter * ref[c : c + 1, :]
                    + leave * ref[COMPS + c : COMPS + c + 1, :]
                    for c in range(COMPS)
                ],
                axis=0,
            )

        x_plus, x_minus = joined(x_plus, ahead_ref), joined(x_minus, behind_ref)
    pad = jnp.zeros((2, cells_z), F32)
    table_ref[...] = split_rows(jnp.concatenate([x_plus, y_plus, corner, pad], axis=0))
    order = lax.broadcasted_iota(jnp.int32, (rows, TILE), 0)
    for t in range(cell_ref.shape[1] // TILE):
        here = slice(t * TILE, (t + 1) * TILE)
        cell = cell_ref[:, here]
        row, column = cell // cells_z, (cell % cells_z).astype(F32)
        fx, fy, fz = (off_ref[d : d + 1, here] for d in range(3))
        found = jnp.dot(table_ref[...], across(column, cells_z), preferred_element_type=F32)
        chosen_ref[here, :] = down(column, cells_z)
        blended = blend_z(found, fz)
        at_row = order == row
        weight = jnp.where(at_row, 1.0 - fy, jnp.where(order == row + 1, fy, 0.0)) * fx
        edge = jnp.where(row == rows - 1, fy, 0.0)
        slot = t * TILE + lax.broadcasted_iota(jnp.int32, (1, TILE), 1)
        remain = slot - RESIDENT
        heading = remain // CAP
        limit = jnp.where(
            heading <= 0,
            count_ref[0, 0, 0],
            jnp.where(heading == 1, count_ref[0, 0, 1], count_ref[0, 0, 2]),
        )
        live = jnp.where((remain < 0) | (remain % CAP < limit), 1.0, 0.0)
        tau = tau_ref[:, here]
        spread = []
        for c in range(COMPS):
            part = jnp.sum(blended[rows * c : rows * (c + 1)] * weight, axis=0, keepdims=True)
            side = blended[count + c : count + c + 1] * (1.0 - fx)
            side = side + blended[count + COMPS + c : count + COMPS + c + 1] * fx
            fluid = near_ref[c : c + 1, here] + part + side * edge
            v = v_ref[c : c + 1, here]
            drag = tau * (fluid - v)
            v = v + step * drag
            v_out_ref[c : c + 1, here] = v * live if last else v
            spread.append(jnp.where(at_row, drag * live * (-COUPLING), 0.0))
        spread = jnp.concatenate(spread, axis=0)
        high = spread.astype(BF16).astype(F32)
        spread_ref[:, here] = jnp.concatenate([high, spread - high], axis=0).astype(BF16)
    pushed = jnp.dot(spread_ref[...], chosen_ref[...], preferred_element_type=F32)

    u = u_ref[...]
    slope_x = (x_plus - x_minus) * (0.5 * STREAM_SCALE)
    slope_z = (pltpu.roll(u, cells_z - 1, 1) - pltpu.roll(u, 1, 1)) * (0.5 * SPAN_SCALE)
    metric = 0.5 * answer_ref[number, :, METRIC : METRIC + 1]
    rhs = []
    for c in range(COMPS):
        own = slice(rows * c, rows * (c + 1))
        field = u[own]
        upper = jnp.concatenate([field[1:], y_plus[c : c + 1]], axis=0)
        lower = jnp.concatenate([y_minus[c : c + 1], field[:-1]], axis=0)
        slope_y = (upper - lower) * metric
        convection = -(
            u[:rows] * slope_x[own] + u[rows : 2 * rows] * slope_y + u[2 * rows :] * slope_z[own]
        )
        force = pushed[own] + pushed[count + rows * c : count + rows * (c + 1)]
        rhs.append(field + step * (convection + force))
    solved = jnp.dot(
        matrix_ref[number, :, 0:count],
        jnp.concatenate(rhs, axis=0),
        precision=lax.Precision.HIGHEST,
        preferred_element_type=F32,
    )
    w_ref[...] = solved[:count]
    pq_ref[0:COMPS, :] = solved[count : count + COMPS]
    for c in range(COMPS):
        pq_ref[COMPS + c : COMPS + c + 1, :] = solved[rows * c : rows * c + 1]
    pq_ref[6:8, :] = jnp.zeros((2, cells_z), F32)
    pq_ref[6:8, 0:128] = scal_ref[number]
    if last:
        leaving_ref[...] = v_out_ref[:, RESIDENT : RESIDENT + CAP]
        pq_ref[8 : 8 + COMPS, :] = v_out_ref[:, RESIDENT + CAP : RESIDENT + 3 * CAP]
        pq_ref[8 + COMPS :, :] = jnp.zeros((8 - COMPS, cells_z), F32)


def join_kernel(number, last, blocks, direct, *refs):
    refs = list(refs)
    take = lambda count: [refs.pop(0) for _ in range(count)]
    here = lax.axis_index("gy")
    if direct:
        sources = take(5)
    else:
        (all_ref,) = take(1)
    w_ref, answer_ref = take(2)
    if last:
        v_ref, from_x_ref, u_ref, moved_ref = take(4)
    else:
        u_ref, ef_ref, ym_ref = take(3)
    if direct:
        (all_ref,) = refs
        own_ref, partner_ref, side_ref, other_ref, far_ref = sources
        odd = here % 2 == 1
        all_ref[here] = own_ref[...]
        all_ref[here ^ 1] = partner_ref[...]
        near = here ^ jnp.where(odd, 4, 2)
        all_ref[near] = side_ref[0]
        all_ref[near ^ 1] = side_ref[1]
        near = here ^ jnp.where(odd, 2, 4)
        all_ref[near ^ 1] = other_ref[0]
        all_ref[near] = other_ref[1]
        all_ref[here ^ 6] = far_ref[0]
        all_ref[here ^ 7] = far_ref[1]
    rows = w_ref.shape[0] // COMPS

    def scal(k, which, row=7):
        return all_ref[k, row : row + 1, which : which + 1]

    zero = jnp.zeros((COMPS, w_ref.shape[1]), F32)
    entering, own_in, at = zero, zero, []
    for k in range(blocks):
        at.append(entering)
        own_in = jnp.where(here == k, entering, own_in)
        entering = all_ref[k, 0:COMPS, :] + scal(k, ENTER, 6) * entering
    leaving, own_out = zero, zero
    for k in reversed(range(blocks)):
        own_out = jnp.where(here == k, leaving, own_out)
        leaving = (
            all_ref[k, COMPS : 2 * COMPS, :] + scal(k, ENTER) * at[k] + scal(k, LEAVE) * leaving
        )
    enter = answer_ref[number, :, ENTER : ENTER + 1]
    leave = answer_ref[number, :, LEAVE : LEAVE + 1]
    for c in range(COMPS):
        own = slice(rows * c, rows * (c + 1))
        u_ref[own, :] = w_ref[own, :] + enter * own_in[c : c + 1] + leave * own_out[c : c + 1]
    below = jnp.maximum(here - 1, 0)
    if last:
        above = jnp.minimum(here + 1, blocks - 1)
        keep_above = jnp.where(here == blocks - 1, 0.0, 1.0).astype(F32)
        keep_below = jnp.where(here == 0, 0.0, 1.0).astype(F32)
        moved_ref[:, :RESIDENT] = v_ref[:, :RESIDENT]
        moved_ref[:, RESIDENT : RESIDENT + CAP] = from_x_ref[...]
        moved_ref[:, RESIDENT + CAP : RESIDENT + 2 * CAP] = (
            all_ref[above, 8 : 8 + COMPS, 0:CAP] * keep_above
        )
        moved_ref[:, RESIDENT + 2 * CAP :] = (
            all_ref[below, 8 : 8 + COMPS, CAP : 2 * CAP] * keep_below
        )
    else:
        ef_ref[0:COMPS, :] = own_in
        ef_ref[COMPS : 2 * COMPS, :] = own_out
        ef_ref[2 * COMPS :, :] = jnp.zeros((2, w_ref.shape[1]), F32)
        for c in range(COMPS):
            ym_ref[c : c + 1, :] = (
                scal(below, PIVOT) * own_in[c : c + 1]
                + scal(below, UPWARD) * u_ref[rows * c : rows * c + 1, :]
            )


def on_device(
    velocity,
    y_metric,
    forward_rate,
    backward_rate,
    pivot_inv,
    particle_vel,
    particle_cell,
    particle_offset,
    inverse_tau,
    outgoing_count,
):
    comps, cells_x, cells_y, cells_z = velocity.shape
    assert (comps, cells_x, cells_y) == (COMPS, 1, 16)
    slots = particle_vel.shape[1]
    size_x, size_y = lax.axis_size("gx"), lax.axis_size("gy")
    ring_x = [(i, (i + 1) % size_x) for i in range(size_x)]
    back_x = [(b, a) for a, b in ring_x]
    ring_y = [(i, (i + 1) % size_y) for i in range(size_y)]
    back_y = [(b, a) for a, b in ring_y]
    flip = lambda bits: [(i, i ^ bits) for i in range(size_y)]
    mixed = [(i, i ^ (4 if i % 2 else 2)) for i in range(size_y)]
    direct = size_y == 8

    u = velocity.reshape(COMPS * cells_y, cells_z)
    first = velocity[:, 0, 0, :]
    final = velocity[:, 0, cells_y - 1, :]
    xp = lax.ppermute(u, "gx", back_x)
    xm = lax.ppermute(u, "gx", ring_x)
    yp = lax.ppermute(first, "gy", back_y)
    ym = lax.ppermute(final, "gy", ring_y)
    ahead = lax.ppermute(yp, "gx", back_x)

    cell = particle_cell.reshape(1, slots)
    tau = inverse_tau.reshape(1, slots)
    like = lambda *shape: jax.ShapeDtypeStruct(shape, F32)
    matrix, answer, scal = call(
        tables_kernel,
        (like(SECTIONS, 56, 128), like(SECTIONS, cells_y, 128), like(SECTIONS, 2, 128)),
        scalars(4),
        "tables",
    )(forward_rate, backward_rate, pivot_inv, y_metric)
    v = particle_vel
    rows = COMPS * cells_y
    field_like, slots_like = like(rows, cells_z), like(COMPS, slots)
    for k in range(SECTIONS):
        last = k == SECTIONS - 1
        near = call(
            own_plane_kernel,
            slots_like,
            whole_in_vmem(3),
            "own_plane",
            [pltpu.VMEM((4 * rows, cells_z), BF16)],
        )(u, cell, particle_offset)
        sides = (u, ym, xp, xm, yp, ahead) + (() if k == 0 else (behind,))
        out = call(
            functools.partial(section_kernel, k, TIME_STEP * SECTION_WEIGHTS[k], last),
            (field_like, like(16 if last else 8, cells_z), slots_like)
            + ((like(COMPS, CAP),) if last else ()),
            scalars(1) + whole_in_vmem(len(sides) + 8),
            "section",
            [
                pltpu.VMEM((4 * (rows + 8), cells_z), BF16),
                pltpu.VMEM((2 * rows, slots), BF16),
                pltpu.VMEM((slots, cells_z), BF16),
            ],
        )(outgoing_count, *sides, cell, particle_offset, tau, v, near, matrix, answer, scal)
        w, pq, v = out[:3]
        if direct:
            partner = lax.ppermute(pq, "gy", flip(1))
            pair = jnp.stack([pq, partner])
            side = lax.ppermute(pair, "gy", mixed)
            far = lax.ppermute(pair, "gy", flip(6))
            other = lax.ppermute(side, "gy", flip(1))
            gathered = (pq, partner, side, other, far)
            scratch = [pltpu.VMEM((size_y,) + pq.shape, F32)]
        else:
            gathered = (lax.all_gather(pq, "gy", axis=0),)
            scratch = []
        if last:
            from_x = lax.ppermute(out[3], "gx", ring_x)
            more, shapes = (v, from_x), (field_like, slots_like)
        else:
            xp = lax.ppermute(w, "gx", back_x)
            xm = lax.ppermute(w, "gx", ring_x)
            more, shapes = (), (field_like, like(8, cells_z), like(COMPS, cells_z))
        joined = call(
            functools.partial(join_kernel, k, last, size_y, direct),
            shapes,
            whole_in_vmem(len(gathered) + 2 + len(more)),
            "join",
            scratch,
        )(*gathered, w, answer, *more)
        if not last:
            u, yp, ym = joined
            ahead = lax.ppermute(yp, "gx", back_x)
            behind = lax.ppermute(yp, "gx", ring_x)
    u, moved = joined
    return (u.reshape(velocity.shape), moved)


def solution(mesh):
    return jax.shard_map(
        on_device,
        mesh=mesh,
        in_specs=(
            P(None, "gx", "gy", None),
            P("gy"),
            P(None, "gy"),
            P(None, "gy"),
            P(None, "gy"),
            P(None, ("gx", "gy")),
            P(("gx", "gy")),
            P(None, ("gx", "gy")),
            P(("gx", "gy")),
            P("gx", "gy", None),
        ),
        out_specs=(P(None, "gx", "gy", None), P(None, ("gx", "gy"))),
        check_vma=False,
    )
```

```python
import functools

import jax
import jax.numpy as jnp
from jax import lax
from jax.experimental import pallas as pl
from jax.experimental.pallas import tpu as pltpu
from jax.sharding import PartitionSpec as P

RESIDENT = 2048
CAP = 512
SECTIONS = 3

SECTION_WEIGHTS = (8.0 / 15.0, 5.0 / 12.0, 3.0 / 4.0)
TIME_STEP = 0.3
STREAM_SCALE = 2.0
SPAN_SCALE = 2.0
COUPLING = 0.5
COMPS = 3
TILE = 512
DEPTH = 256
VMEM_LIMIT = 32 * 1024 * 1024
ENTER, LEAVE, PIVOT, UPWARD, METRIC = range(16, 21)

F32 = jnp.float32
BF16 = jnp.bfloat16


def call(kernel, out_shape, in_specs, name, scratch_shapes=()):
    several = isinstance(out_shape, tuple)
    out_specs = whole_in_vmem(len(out_shape)) if several else whole_in_vmem(1)[0]
    return pl.pallas_call(
        kernel,
        out_shape=out_shape,
        in_specs=in_specs,
        out_specs=tuple(out_specs) if several else out_specs,
        scratch_shapes=scratch_shapes,
        compiler_params=pltpu.CompilerParams(vmem_limit_bytes=VMEM_LIMIT),
        name=name,
    )


def whole_in_vmem(count):
    return [pl.BlockSpec(memory_space=pltpu.VMEM)] * count


def scalars(count):
    return [pl.BlockSpec(memory_space=pltpu.SMEM)] * count


def across(row, depth):
    width = row.shape[1]
    shape = (DEPTH // 16, 16, width)
    order = lax.broadcasted_iota(jnp.int32, shape, 0) * 16 + lax.broadcasted_iota(jnp.int32, shape, 1)
    order = order.astype(F32).astype(BF16)
    one, none = jnp.ones((), BF16), jnp.zeros((), BF16)
    parts = []
    for k in range(depth // DEPTH):
        wanted = jnp.broadcast_to(row - float(DEPTH * k), (16, width)).astype(BF16)
        parts.append(jnp.where(order == wanted[None], one, none).reshape(DEPTH, width))
    return jnp.concatenate(parts, axis=0)


def down(row, depth):
    width = row.shape[1]
    order = lax.broadcasted_iota(jnp.int32, (width, DEPTH), 1).astype(F32).astype(BF16)
    one, none = jnp.ones((), BF16), jnp.zeros((), BF16)
    column = jnp.broadcast_to(row, (8, width)).T[:, 0:1]
    parts = []
    for k in range(depth // DEPTH):
        wanted = jnp.broadcast_to(column - float(DEPTH * k), (width, DEPTH)).astype(BF16)
        parts.append(jnp.where(order == wanted, one, none))
    return jnp.concatenate(parts, axis=1)


def split_rows(rows):
    length = rows.shape[1]
    high = rows.astype(BF16).astype(F32)
    low = rows - high
    ahead = [pltpu.roll(part, length - 1, 1) for part in (high, low)]
    return jnp.concatenate([high, low] + ahead, axis=0).astype(BF16)


def blend_z(values, fz):
    rows = values.shape[0] // 4
    near = values[:rows] + values[rows : 2 * rows]
    far = values[2 * rows : 3 * rows] + values[3 * rows :]
    return near * (1.0 - fz) + far * fz


def tables_kernel(down_ref, up_ref, scale_ref, metric_ref, matrix_ref, answer_ref, scal_ref):
    sections, rows = down_ref.shape
    lane = lax.broadcasted_iota(jnp.int32, (1, 128), 1)
    at = lambda place: jnp.where(lane == place, 1.0, 0.0)
    matrix_ref[...] = jnp.zeros_like(matrix_ref)
    scal_ref[...] = jnp.zeros_like(scal_ref)
    for k in range(sections):
        lower = []
        row = at(ENTER)
        for i in range(rows):
            row = down_ref[k, i] * row + at(i)
            lower.append(row)
        last = jnp.where(lane < rows, row, 0.0)
        for c in range(COMPS):
            place = COMPS * rows + c
            matrix_ref[k, place : place + 1, :] = pltpu.roll(last, rows * c, 1)
        scal_ref[k, 0:1, :] = row
        row = at(LEAVE)
        for i in reversed(range(rows)):
            row = scale_ref[k, i] * lower[i] + up_ref[k, i] * row
            inner = jnp.where(lane < rows, row, 0.0)
            for c in range(COMPS):
                place = rows * c + i
                matrix_ref[k, place : place + 1, :] = inner if c == 0 else pltpu.roll(inner, rows * c, 1)
            answer_ref[k, i : i + 1, :] = row + metric_ref[i] * at(METRIC)
        scal_ref[k, 1:2, :] = (
            row + scale_ref[k, rows - 1] * at(PIVOT) + up_ref[k, rows - 1] * at(UPWARD)
        )


def own_plane_kernel(u_ref, cell_ref, off_ref, out_ref, table_ref):
    cells_z = u_ref.shape[1]
    rows = u_ref.shape[0] // COMPS
    table_ref[...] = split_rows(u_ref[...])
    order = lax.broadcasted_iota(jnp.int32, (rows, TILE), 0)
    for t in range(cell_ref.shape[1] // TILE):
        here = slice(t * TILE, (t + 1) * TILE)
        cell = cell_ref[:, here]
        row = cell // cells_z
        fx, fy, fz = (off_ref[d : d + 1, here] for d in range(3))
        chosen = across((cell % cells_z).astype(F32), cells_z)
        blended = blend_z(jnp.dot(table_ref[...], chosen, preferred_element_type=F32), fz)
        weight = jnp.where(order == row, 1.0 - fy, jnp.where(order == row + 1, fy, 0.0))
        weight = weight * (1.0 - fx)
        for c in range(COMPS):
            part = blended[rows * c : rows * (c + 1)] * weight
            out_ref[c : c + 1, here] = jnp.sum(part, axis=0, keepdims=True)


def section_kernel(number, step, last, *refs):
    first = number == 0
    refs = list(refs)
    take = lambda count: [refs.pop(0) for _ in range(count)]
    count_ref, u_ref, ym_ref, near_x_ref, far_x_ref, yp_ref, near_ef_ref, far_ef_ref = take(8)
    cell_ref, off_ref, tau_ref, v_ref, near_ref, matrix_ref, answer_ref, scal_ref = take(8)
    w_ref, pq_ref, v_out_ref = take(3)
    if last:
        leaving_x_ref, leaving_y_ref = take(2)
    table_ref, spread_ref, chosen_ref = refs

    cells_z = u_ref.shape[1]
    rows = u_ref.shape[0] // COMPS
    count = COMPS * rows
    position = lax.axis_index("gy")
    top = jnp.where(position == lax.axis_size("gy") - 1, 0.0, 1.0).astype(F32)
    bottom = jnp.where(position == 0, 0.0, 1.0).astype(F32)
    y_minus = ym_ref[...] * bottom
    even = lax.axis_index("gx") % 2 == 0

    def sides(one, other):
        return jnp.where(even, one, other), jnp.where(even, other, one)

    x_plus, x_minus = sides(near_x_ref[...], far_x_ref[...])
    ahead, behind = sides(near_ef_ref[...], far_ef_ref[...])
    if first:
        y_plus = yp_ref[...] * top
        corner = ahead * top
    else:
        y_plus = yp_ref[COMPS : 2 * COMPS, :]
        corner = ahead[COMPS : 2 * COMPS]
        enter = answer_ref[number - 1, :, ENTER : ENTER + 1]
        leave = answer_ref[number - 1, :, LEAVE : LEAVE + 1]

        def joined(plane, ef):
            return jnp.concatenate(
                [
                    plane[rows * c : rows * (c + 1)]
                    + enter * ef[c : c + 1]
                    + leave * ef[COMPS + c : COMPS + c + 1]
                    for c in range(COMPS)
                ],
                axis=0,
            )

        x_plus, x_minus = joined(x_plus, ahead), joined(x_minus, behind)
    pad = jnp.zeros((2, cells_z), F32)
    table_ref[...] = split_rows(jnp.concatenate([x_plus, y_plus, corner, pad], axis=0))
    order = lax.broadcasted_iota(jnp.int32, (rows, TILE), 0)
    for t in range(cell_ref.shape[1] // TILE):
        here = slice(t * TILE, (t + 1) * TILE)
        cell = cell_ref[:, here]
        row, column = cell // cells_z, (cell % cells_z).astype(F32)
        fx, fy, fz = (off_ref[d : d + 1, here] for d in range(3))
        found = jnp.dot(table_ref[...], across(column, cells_z), preferred_element_type=F32)
        chosen_ref[here, :] = down(column, cells_z)
        blended = blend_z(found, fz)
        at_row = order == row
        weight = jnp.where(at_row, 1.0 - fy, jnp.where(order == row + 1, fy, 0.0)) * fx
        edge = jnp.where(row == rows - 1, fy, 0.0)
        slot = t * TILE + lax.broadcasted_iota(jnp.int32, (1, TILE), 1)
        remain = slot - RESIDENT
        heading = remain // CAP
        limit = jnp.where(
            heading <= 0,
            count_ref[0, 0, 0],
            jnp.where(heading == 1, count_ref[0, 0, 1], count_ref[0, 0, 2]),
        )
        live = jnp.where((remain < 0) | (remain % CAP < limit), 1.0, 0.0)
        tau = tau_ref[:, here]
        spread = []
        for c in range(COMPS):
            part = jnp.sum(blended[rows * c : rows * (c + 1)] * weight, axis=0, keepdims=True)
            side = blended[count + c : count + c + 1] * (1.0 - fx)
            side = side + blended[count + COMPS + c : count + COMPS + c + 1] * fx
            fluid = near_ref[c : c + 1, here] + part + side * edge
            v = v_ref[c : c + 1, here]
            drag = tau * (fluid - v)
            v = v + step * drag
            v_out_ref[c : c + 1, here] = v * live if last else v
            spread.append(jnp.where(at_row, drag * live * (-COUPLING), 0.0))
        spread = jnp.concatenate(spread, axis=0)
        high = spread.astype(BF16).astype(F32)
        spread_ref[:, here] = jnp.concatenate([high, spread - high], axis=0).astype(BF16)
    pushed = jnp.dot(spread_ref[...], chosen_ref[...], preferred_element_type=F32)

    u = u_ref[...]
    slope_x = (x_plus - x_minus) * (0.5 * STREAM_SCALE)
    slope_z = (pltpu.roll(u, cells_z - 1, 1) - pltpu.roll(u, 1, 1)) * (0.5 * SPAN_SCALE)
    metric = 0.5 * answer_ref[number, :, METRIC : METRIC + 1]
    rhs = []
    for c in range(COMPS):
        own = slice(rows * c, rows * (c + 1))
        field = u[own]
        upper = jnp.concatenate([field[1:], y_plus[c : c + 1]], axis=0)
        lower = jnp.concatenate([y_minus[c : c + 1], field[:-1]], axis=0)
        slope_y = (upper - lower) * metric
        convection = -(
            u[:rows] * slope_x[own] + u[rows : 2 * rows] * slope_y + u[2 * rows :] * slope_z[own]
        )
        force = pushed[own] + pushed[count + rows * c : count + rows * (c + 1)]
        rhs.append(field + step * (convection + force))
    solved = jnp.dot(
        matrix_ref[number, :, 0:count],
        jnp.concatenate(rhs, axis=0),
        precision=lax.Precision.HIGHEST,
        preferred_element_type=F32,
    )
    w_ref[...] = solved[:count]
    pq_ref[0:COMPS, :] = solved[count : count + COMPS]
    for c in range(COMPS):
        pq_ref[COMPS + c : COMPS + c + 1, :] = solved[rows * c : rows * c + 1]
    pq_ref[6:8, :] = jnp.zeros((2, cells_z), F32)
    pq_ref[6:8, 0:128] = scal_ref[number]
    if last:
        leaving_y_ref[...] = v_out_ref[:, RESIDENT + CAP : RESIDENT + 3 * CAP]
        leaving_x_ref[...] = v_out_ref[:, RESIDENT : RESIDENT + CAP]


def join_kernel(number, last, blocks, direct, *refs):
    refs = list(refs)
    take = lambda count: [refs.pop(0) for _ in range(count)]
    here = lax.axis_index("gy")
    if direct:
        sources = take(5)
    else:
        (all_ref,) = take(1)
    w_ref, answer_ref = take(2)
    if last:
        v_ref, from_x_ref, chip_ref, beside_ref, u_ref, moved_ref = take(6)
    else:
        u_ref, ef_ref, ym_ref = take(3)
    if direct:
        (all_ref,) = refs
        own_ref, partner_ref, side_ref, other_ref, far_ref = sources
        odd = here % 2 == 1
        all_ref[here] = own_ref[...]
        all_ref[here ^ 1] = partner_ref[...]
        near = here ^ jnp.where(odd, 4, 2)
        all_ref[near] = side_ref[0]
        all_ref[near ^ 1] = side_ref[1]
        near = here ^ jnp.where(odd, 2, 4)
        all_ref[near ^ 1] = other_ref[0]
        all_ref[near] = other_ref[1]
        all_ref[here ^ 6] = far_ref[0]
        all_ref[here ^ 7] = far_ref[1]
    rows = w_ref.shape[0] // COMPS

    def scal(k, which, row=7):
        return all_ref[k, row : row + 1, which : which + 1]

    zero = jnp.zeros((COMPS, w_ref.shape[1]), F32)
    entering, own_in, at = zero, zero, []
    for k in range(blocks):
        at.append(entering)
        own_in = jnp.where(here == k, entering, own_in)
        entering = all_ref[k, 0:COMPS, :] + scal(k, ENTER, 6) * entering
    leaving, own_out = zero, zero
    for k in reversed(range(blocks)):
        own_out = jnp.where(here == k, leaving, own_out)
        leaving = (
            all_ref[k, COMPS : 2 * COMPS, :] + scal(k, ENTER) * at[k] + scal(k, LEAVE) * leaving
        )
    enter = answer_ref[number, :, ENTER : ENTER + 1]
    leave = answer_ref[number, :, LEAVE : LEAVE + 1]
    for c in range(COMPS):
        own = slice(rows * c, rows * (c + 1))
        u_ref[own, :] = w_ref[own, :] + enter * own_in[c : c + 1] + leave * own_out[c : c + 1]
    below = jnp.maximum(here - 1, 0)
    if last:
        even = here % 2 == 0
        keep_above = jnp.where(here == blocks - 1, 0.0, 1.0).astype(F32)
        keep_below = jnp.where(here == 0, 0.0, 1.0).astype(F32)
        chip, beside = chip_ref[...], beside_ref[...]
        moved_ref[:, :RESIDENT] = v_ref[:, :RESIDENT]
        moved_ref[:, RESIDENT : RESIDENT + CAP] = from_x_ref[...]
        moved_ref[:, RESIDENT + CAP : RESIDENT + 2 * CAP] = (
            jnp.where(even, chip, beside)[:, :CAP] * keep_above
        )
        moved_ref[:, RESIDENT + 2 * CAP :] = jnp.where(even, beside, chip)[:, CAP:] * keep_below
    else:
        ef_ref[0:COMPS, :] = own_in
        ef_ref[COMPS : 2 * COMPS, :] = own_out
        ef_ref[2 * COMPS :, :] = jnp.zeros((2, w_ref.shape[1]), F32)
        for c in range(COMPS):
            ym_ref[c : c + 1, :] = (
                scal(below, PIVOT) * own_in[c : c + 1]
                + scal(below, UPWARD) * u_ref[rows * c : rows * c + 1, :]
            )


def on_device(
    velocity,
    y_metric,
    forward_rate,
    backward_rate,
    pivot_inv,
    particle_vel,
    particle_cell,
    particle_offset,
    inverse_tau,
    outgoing_count,
):
    comps, cells_x, cells_y, cells_z = velocity.shape
    assert (comps, cells_x, cells_y) == (COMPS, 1, 16)
    slots = particle_vel.shape[1]
    size_x, size_y = lax.axis_size("gx"), lax.axis_size("gy")
    assert size_x % 2 == 0 and size_y % 2 == 0
    ring_x = [(i, (i + 1) % size_x) for i in range(size_x)]
    next_to = [(i, (i + (1 if i % 2 else -1)) % size_y) for i in range(size_y)]
    same_pair = [(i, i ^ 1) for i in range(size_x)]
    next_pair = [(i, (i + (1 if i % 2 else -1)) % size_x) for i in range(size_x)]

    def both_sides(block):
        far = lax.ppermute(block, "gx", next_pair)
        return lax.ppermute(block, "gx", same_pair), far

    ring_y = [(i, (i + 1) % size_y) for i in range(size_y)]
    back_y = [(b, a) for a, b in ring_y]
    flip = lambda bits: [(i, i ^ bits) for i in range(size_y)]
    mixed = [(i, i ^ (4 if i % 2 else 2)) for i in range(size_y)]
    direct = size_y == 8

    u = velocity.reshape(COMPS * cells_y, cells_z)
    first = velocity[:, 0, 0, :]
    final = velocity[:, 0, cells_y - 1, :]
    planes = both_sides(u)
    yp = lax.ppermute(first, "gy", back_y)
    ym = lax.ppermute(final, "gy", ring_y)
    edges = both_sides(yp)

    cell = particle_cell.reshape(1, slots)
    tau = inverse_tau.reshape(1, slots)
    like = lambda *shape: jax.ShapeDtypeStruct(shape, F32)
    matrix, answer, scal = call(
        tables_kernel,
        (like(SECTIONS, 56, 128), like(SECTIONS, cells_y, 128), like(SECTIONS, 2, 128)),
        scalars(4),
        "tables",
    )(forward_rate, backward_rate, pivot_inv, y_metric)
    v = particle_vel
    rows = COMPS * cells_y
    field_like, slots_like = like(rows, cells_z), like(COMPS, slots)
    for k in range(SECTIONS):
        last = k == SECTIONS - 1
        near = call(
            own_plane_kernel,
            slots_like,
            whole_in_vmem(3),
            "own_plane",
            [pltpu.VMEM((4 * rows, cells_z), BF16)],
        )(u, cell, particle_offset)
        sides = (u, ym, *planes, yp, *edges)
        out = call(
            functools.partial(section_kernel, k, TIME_STEP * SECTION_WEIGHTS[k], last),
            (field_like, like(8, cells_z), slots_like)
            + ((like(COMPS, CAP), like(COMPS, 2 * CAP)) if last else ()),
            scalars(1) + whole_in_vmem(len(sides) + 8),
            "section",
            [
                pltpu.VMEM((4 * (rows + 8), cells_z), BF16),
                pltpu.VMEM((2 * rows, slots), BF16),
                pltpu.VMEM((slots, cells_z), BF16),
            ],
        )(outgoing_count, *sides, cell, particle_offset, tau, v, near, matrix, answer, scal)
        w, pq, v = out[:3]
        if last:
            from_x = lax.ppermute(out[3], "gx", ring_x)
            chip = lax.ppermute(out[4], "gy", flip(1))
            beside = lax.ppermute(out[4], "gy", next_to)
        if direct:
            partner = lax.ppermute(pq, "gy", flip(1))
            pair = jnp.stack([pq, partner])
            side = lax.ppermute(pair, "gy", mixed)
            far = lax.ppermute(pair, "gy", flip(6))
            if last:
                side, from_x, beside = lax.optimization_barrier((side, from_x, beside))
            other = lax.ppermute(side, "gy", flip(1))
            gathered = (pq, partner, side, other, far)
            scratch = [pltpu.VMEM((size_y,) + pq.shape, F32)]
        else:
            gathered = (lax.all_gather(pq, "gy", axis=0),)
            scratch = []
        if last:
            more, shapes = (v, from_x, chip, beside), (field_like, slots_like)
        else:
            planes = both_sides(w)
            more, shapes = (), (field_like, like(8, cells_z), like(COMPS, cells_z))
        joined = call(
            functools.partial(join_kernel, k, last, size_y, direct),
            shapes,
            whole_in_vmem(len(gathered) + 2 + len(more)),
            "join",
            scratch,
        )(*gathered, w, answer, *more)
        if not last:
            u, yp, ym = joined
            edges = both_sides(yp)
    u, moved = joined
    return (u.reshape(velocity.shape), moved)


def solution(mesh):
    return jax.shard_map(
        on_device,
        mesh=mesh,
        in_specs=(
            P(None, "gx", "gy", None),
            P("gy"),
            P(None, "gy"),
            P(None, "gy"),
            P(None, "gy"),
            P(None, ("gx", "gy")),
            P(("gx", "gy")),
            P(None, ("gx", "gy")),
            P(("gx", "gy")),
            P("gx", "gy", None),
        ),
        out_specs=(P(None, "gx", "gy", None), P(None, ("gx", "gy"))),
        check_vma=False,
    )
```

```python
import functools

import jax
import jax.numpy as jnp
from jax import lax
from jax.experimental import pallas as pl
from jax.experimental.pallas import tpu as pltpu
from jax.sharding import PartitionSpec as P

RESIDENT = 2048
CAP = 512
SECTIONS = 3

SECTION_WEIGHTS = (8.0 / 15.0, 5.0 / 12.0, 3.0 / 4.0)
TIME_STEP = 0.3
STREAM_SCALE = 2.0
SPAN_SCALE = 2.0
COUPLING = 0.5
COMPS = 3
TILE = 512
DEPTH = 256
VMEM_LIMIT = 32 * 1024 * 1024
ENTER, LEAVE, PIVOT, UPWARD, METRIC = range(16, 21)

F32 = jnp.float32
BF16 = jnp.bfloat16


def call(kernel, out_shape, in_specs, name, scratch_shapes=()):
    several = isinstance(out_shape, tuple)
    out_specs = whole_in_vmem(len(out_shape)) if several else whole_in_vmem(1)[0]
    return pl.pallas_call(
        kernel,
        out_shape=out_shape,
        in_specs=in_specs,
        out_specs=tuple(out_specs) if several else out_specs,
        scratch_shapes=scratch_shapes,
        compiler_params=pltpu.CompilerParams(vmem_limit_bytes=VMEM_LIMIT),
        name=name,
    )


def whole_in_vmem(count):
    return [pl.BlockSpec(memory_space=pltpu.VMEM)] * count


def scalars(count):
    return [pl.BlockSpec(memory_space=pltpu.SMEM)] * count


def across(row, depth):
    width = row.shape[1]
    shape = (DEPTH // 16, 16, width)
    order = lax.broadcasted_iota(jnp.int32, shape, 0) * 16 + lax.broadcasted_iota(jnp.int32, shape, 1)
    order = order.astype(F32).astype(BF16)
    one, none = jnp.ones((), BF16), jnp.zeros((), BF16)
    parts = []
    for k in range(depth // DEPTH):
        wanted = jnp.broadcast_to(row - float(DEPTH * k), (16, width)).astype(BF16)
        parts.append(jnp.where(order == wanted[None], one, none).reshape(DEPTH, width))
    return jnp.concatenate(parts, axis=0)


def down(row):
    width = row.shape[1]
    order = lax.broadcasted_iota(jnp.int32, (width, DEPTH), 1).astype(F32).astype(BF16)
    column = jnp.broadcast_to(row, (8, width)).T[:, 0:1]
    wanted = jnp.broadcast_to(column, (width, DEPTH)).astype(BF16)
    return jnp.where(order == wanted, jnp.ones((), BF16), jnp.zeros((), BF16))


def spread_out(values, group, groups):
    width = group.shape[1]
    shape = (groups // 16, 16, width)
    order = lax.broadcasted_iota(jnp.int32, shape, 0) * 16 + lax.broadcasted_iota(jnp.int32, shape, 1)
    order = order.astype(F32).astype(BF16)
    hit = order == jnp.broadcast_to(group.astype(F32), (16, width)).astype(BF16)[None]
    parts = []
    for value in values:
        value = jnp.broadcast_to(value, (16, width)).astype(BF16)[None]
        parts.append(jnp.where(hit, value, jnp.zeros((), BF16)).reshape(groups, width))
    return jnp.concatenate(parts, axis=0)


def split_rows(rows):
    length = rows.shape[1]
    high = rows.astype(BF16).astype(F32)
    low = rows - high
    ahead = [pltpu.roll(part, length - 1, 1) for part in (high, low)]
    return jnp.concatenate([high, low] + ahead, axis=0).astype(BF16)


def blend_z(values, fz):
    rows = values.shape[0] // 4
    near = values[:rows] + values[rows : 2 * rows]
    far = values[2 * rows : 3 * rows] + values[3 * rows :]
    return near * (1.0 - fz) + far * fz


def tables_kernel(
    down_ref, up_ref, scale_ref, metric_ref, count_ref, matrix_ref, answer_ref, scal_ref, live_ref
):
    slot = lax.broadcasted_iota(jnp.int32, live_ref.shape, 1)
    remain = slot - RESIDENT
    heading = remain // CAP
    limit = jnp.where(
        heading <= 0,
        count_ref[0, 0, 0],
        jnp.where(heading == 1, count_ref[0, 0, 1], count_ref[0, 0, 2]),
    )
    live_ref[...] = jnp.where((remain < 0) | (remain % CAP < limit), 1.0, 0.0)
    sections, rows = down_ref.shape
    lane = lax.broadcasted_iota(jnp.int32, (1, 128), 1)
    at = lambda place: jnp.where(lane == place, 1.0, 0.0)
    matrix_ref[...] = jnp.zeros_like(matrix_ref)
    scal_ref[...] = jnp.zeros_like(scal_ref)
    for k in range(sections):
        lower = []
        row = at(ENTER)
        for i in range(rows):
            row = down_ref[k, i] * row + at(i)
            lower.append(row)
        last = jnp.where(lane < rows, row, 0.0)
        for c in range(COMPS):
            place = COMPS * rows + c
            matrix_ref[k, place : place + 1, :] = pltpu.roll(last, rows * c, 1)
        scal_ref[k, 0:1, :] = row
        row = at(LEAVE)
        for i in reversed(range(rows)):
            row = scale_ref[k, i] * lower[i] + up_ref[k, i] * row
            inner = jnp.where(lane < rows, row, 0.0)
            for c in range(COMPS):
                place = rows * c + i
                matrix_ref[k, place : place + 1, :] = inner if c == 0 else pltpu.roll(inner, rows * c, 1)
            answer_ref[k, i : i + 1, :] = row + metric_ref[i] * at(METRIC)
        scal_ref[k, 1:2, :] = (
            row + scale_ref[k, rows - 1] * at(PIVOT) + up_ref[k, rows - 1] * at(UPWARD)
        )


def own_plane_kernel(u_ref, cell_ref, off_ref, out_ref, table_ref):
    cells_z = u_ref.shape[1]
    rows = u_ref.shape[0] // COMPS
    table_ref[...] = split_rows(u_ref[...])
    order = lax.broadcasted_iota(jnp.int32, (rows, TILE), 0)
    for t in range(cell_ref.shape[1] // TILE):
        here = slice(t * TILE, (t + 1) * TILE)
        cell = cell_ref[:, here]
        row = cell // cells_z
        fx, fy, fz = (off_ref[d : d + 1, here] for d in range(3))
        chosen = across((cell % cells_z).astype(F32), cells_z)
        blended = blend_z(jnp.dot(table_ref[...], chosen, preferred_element_type=F32), fz)
        weight = jnp.where(order == row, 1.0 - fy, jnp.where(order == row + 1, fy, 0.0))
        weight = weight * (1.0 - fx)
        for c in range(COMPS):
            part = blended[rows * c : rows * (c + 1)] * weight
            out_ref[c : c + 1, here] = jnp.sum(part, axis=0, keepdims=True)


def section_kernel(number, step, last, *refs):
    first = number == 0
    refs = list(refs)
    take = lambda count: [refs.pop(0) for _ in range(count)]
    u_ref, ym_ref, near_x_ref, far_x_ref, yp_ref, near_ef_ref, far_ef_ref = take(7)
    cell_ref, off_ref, tau_ref, live_ref, v_ref, near_ref, matrix_ref, answer_ref, scal_ref = take(9)
    w_ref, pq_ref, v_out_ref = take(3)
    leaving_ref = refs.pop(0) if last else None
    table_ref, spread_ref, chosen_ref = refs

    cells_z = u_ref.shape[1]
    rows = u_ref.shape[0] // COMPS
    count = COMPS * rows
    groups = rows * (cells_z // DEPTH)
    position = lax.axis_index("gy")
    top = jnp.where(position == lax.axis_size("gy") - 1, 0.0, 1.0).astype(F32)
    bottom = jnp.where(position == 0, 0.0, 1.0).astype(F32)
    y_minus = ym_ref[...] * bottom
    even = lax.axis_index("gx") % 2 == 0

    def sides(one, other):
        return jnp.where(even, one, other), jnp.where(even, other, one)

    x_plus, x_minus = sides(near_x_ref[...], far_x_ref[...])
    ahead, behind = sides(near_ef_ref[...], far_ef_ref[...])
    if first:
        y_plus = yp_ref[...] * top
        corner = ahead * top
    else:
        y_plus = yp_ref[COMPS : 2 * COMPS, :]
        corner = ahead[COMPS : 2 * COMPS]
        enter = answer_ref[number - 1, :, ENTER : ENTER + 1]
        leave = answer_ref[number - 1, :, LEAVE : LEAVE + 1]

        def joined(plane, ef):
            return jnp.concatenate(
                [
                    plane[rows * c : rows * (c + 1)]
                    + enter * ef[c : c + 1]
                    + leave * ef[COMPS + c : COMPS + c + 1]
                    for c in range(COMPS)
                ],
                axis=0,
            )

        x_plus, x_minus = joined(x_plus, ahead), joined(x_minus, behind)
    pad = jnp.zeros((2, cells_z), F32)
    table_ref[...] = split_rows(jnp.concatenate([x_plus, y_plus, corner, pad], axis=0))
    order = lax.broadcasted_iota(jnp.int32, (rows, TILE), 0)
    for t in range(cell_ref.shape[1] // TILE):
        here = slice(t * TILE, (t + 1) * TILE)
        cell = cell_ref[:, here]
        row, place = cell // cells_z, cell % cells_z
        column = place.astype(F32)
        fx, fy, fz = (off_ref[d : d + 1, here] for d in range(3))
        found = jnp.dot(table_ref[...], across(column, cells_z), preferred_element_type=F32)
        chosen_ref[here, :] = down((place % DEPTH).astype(F32))
        blended = blend_z(found, fz)
        weight = jnp.where(order == row, 1.0 - fy, jnp.where(order == row + 1, fy, 0.0)) * fx
        edge = jnp.where(row == rows - 1, fy, 0.0)
        live = live_ref[:, here]
        tau = tau_ref[:, here]
        pushes = []
        for c in range(COMPS):
            part = jnp.sum(blended[rows * c : rows * (c + 1)] * weight, axis=0, keepdims=True)
            side = blended[count + c : count + c + 1] * (1.0 - fx)
            side = side + blended[count + COMPS + c : count + COMPS + c + 1] * fx
            fluid = near_ref[c : c + 1, here] + part + side * edge
            v = v_ref[c : c + 1, here]
            drag = tau * (fluid - v)
            v = v + step * drag
            v_out_ref[c : c + 1, here] = v * live if last else v
            pushes.append(drag * live * (-COUPLING))
        high = [push.astype(BF16).astype(F32) for push in pushes]
        low = [push - part for push, part in zip(pushes, high)]
        spread_ref[:, here] = spread_out(high + low, place // DEPTH * rows + row, groups)
    pushed = jnp.dot(spread_ref[...], chosen_ref[...], preferred_element_type=F32)

    u = u_ref[...]
    slope_x = (x_plus - x_minus) * (0.5 * STREAM_SCALE)
    slope_z = (pltpu.roll(u, cells_z - 1, 1) - pltpu.roll(u, 1, 1)) * (0.5 * SPAN_SCALE)
    metric = 0.5 * answer_ref[number, :, METRIC : METRIC + 1]
    rhs = []
    for c in range(COMPS):
        own = slice(rows * c, rows * (c + 1))
        field = u[own]
        upper = jnp.concatenate([field[1:], y_plus[c : c + 1]], axis=0)
        lower = jnp.concatenate([y_minus[c : c + 1], field[:-1]], axis=0)
        slope_y = (upper - lower) * metric
        convection = -(
            u[:rows] * slope_x[own] + u[rows : 2 * rows] * slope_y + u[2 * rows :] * slope_z[own]
        )
        pieces = []
        for k in range(cells_z // DEPTH):
            high, low = (groups * (c + COMPS * i) + rows * k for i in range(2))
            pieces.append(pushed[high : high + rows] + pushed[low : low + rows])
        force = jnp.concatenate(pieces, axis=1)
        rhs.append(field + step * (convection + force))
    solved = jnp.dot(
        matrix_ref[number, :, 0:count],
        jnp.concatenate(rhs, axis=0),
        precision=lax.Precision.HIGHEST,
        preferred_element_type=F32,
    )
    w_ref[...] = solved[:count]
    pq_ref[0:COMPS, :] = solved[count : count + COMPS]
    for c in range(COMPS):
        pq_ref[COMPS + c : COMPS + c + 1, :] = solved[rows * c : rows * c + 1]
    pq_ref[6:, :] = jnp.zeros((pq_ref.shape[0] - 6, cells_z), F32)
    if first:
        for k in range(scal_ref.shape[0]):
            pq_ref[6:8, 128 * k : 128 * (k + 1)] = scal_ref[k]
    if last:
        leaving_ref[...] = v_out_ref[:, RESIDENT : RESIDENT + CAP]
        lower = v_out_ref[:, RESIDENT + CAP : RESIDENT + 2 * CAP]
        upper = v_out_ref[:, RESIDENT + 2 * CAP :]
        even = position % 2 == 0
        for place, part in ((6, jnp.where(even, lower, upper)), (8, jnp.where(even, upper, lower))):
            pq_ref[place : place + 1, 0:CAP] = part[0:1]
            pq_ref[place : place + 1, CAP : 2 * CAP] = part[1:2]
            pq_ref[place + 1 : place + 2, 0:CAP] = part[2:3]


def join_kernel(number, last, blocks, direct, *refs):
    refs = list(refs)
    take = lambda count: [refs.pop(0) for _ in range(count)]
    here = lax.axis_index("gy")
    if direct:
        sources = take(5)
    else:
        (all_ref,) = take(1)
    w_ref, answer_ref = take(2)
    if number > 0:
        (known_ref,) = take(1)
    if last:
        v_ref, from_x_ref, u_ref, moved_ref = take(4)
    else:
        u_ref, ef_ref, ym_ref = take(3)
        if number == 0:
            (known_ref,) = take(1)
    if direct:
        (all_ref,) = refs
        own_ref, partner_ref, side_ref, other_ref, far_ref = sources
        odd = here % 2 == 1
        all_ref[here] = own_ref[0:8, :]
        all_ref[here ^ 1] = partner_ref[0:8, :]
        near = here ^ jnp.where(odd, 4, 2)
        all_ref[near] = side_ref[0]
        all_ref[near ^ 1] = side_ref[1]
        near = here ^ jnp.where(odd, 2, 4)
        all_ref[near ^ 1] = other_ref[0]
        all_ref[near] = other_ref[1]
        all_ref[here ^ 6] = far_ref[0]
        all_ref[here ^ 7] = far_ref[1]
    rows = w_ref.shape[0] // COMPS
    if number == 0:
        known_ref[...] = all_ref[:, 6:8, 0 : known_ref.shape[2]]

    def scal(k, which, row=1):
        place = 128 * number + which
        return known_ref[k, row : row + 1, place : place + 1]

    zero = jnp.zeros((COMPS, w_ref.shape[1]), F32)
    entering, own_in, at = zero, zero, []
    for k in range(blocks):
        at.append(entering)
        own_in = jnp.where(here == k, entering, own_in)
        entering = all_ref[k, 0:COMPS, :] + scal(k, ENTER, 0) * entering
    leaving, own_out = zero, zero
    for k in reversed(range(blocks)):
        own_out = jnp.where(here == k, leaving, own_out)
        leaving = (
            all_ref[k, COMPS : 2 * COMPS, :] + scal(k, ENTER) * at[k] + scal(k, LEAVE) * leaving
        )
    enter = answer_ref[number, :, ENTER : ENTER + 1]
    leave = answer_ref[number, :, LEAVE : LEAVE + 1]
    for c in range(COMPS):
        own = slice(rows * c, rows * (c + 1))
        u_ref[own, :] = w_ref[own, :] + enter * own_in[c : c + 1] + leave * own_out[c : c + 1]
    below = jnp.maximum(here - 1, 0)
    if last:
        even = here % 2 == 0
        keep_above = jnp.where(here == blocks - 1, 0.0, 1.0).astype(F32)
        keep_below = jnp.where(here == 0, 0.0, 1.0).astype(F32)
        across_chips = jnp.where(even, below, jnp.minimum(here + 1, blocks - 1))
        moved_ref[:, :RESIDENT] = v_ref[:, :RESIDENT]
        moved_ref[:, RESIDENT : RESIDENT + CAP] = from_x_ref[...]
        for c in range(COMPS):
            row, lanes = c // 2, slice(CAP * (c % 2), CAP * (c % 2) + CAP)
            beside = all_ref[across_chips, 6 + row : 7 + row, lanes]
            if direct:
                chip = partner_ref[8 + row : 9 + row, lanes]
            else:
                chip = all_ref[here ^ 1, 8 + row : 9 + row, lanes]
            own = slice(c, c + 1)
            moved_ref[own, RESIDENT + CAP : RESIDENT + 2 * CAP] = (
                jnp.where(even, chip, beside) * keep_above
            )
            moved_ref[own, RESIDENT + 2 * CAP :] = jnp.where(even, beside, chip) * keep_below
    else:
        ef_ref[0:COMPS, :] = own_in
        ef_ref[COMPS : 2 * COMPS, :] = own_out
        ef_ref[2 * COMPS :, :] = jnp.zeros((2, w_ref.shape[1]), F32)
        for c in range(COMPS):
            ym_ref[c : c + 1, :] = (
                scal(below, PIVOT) * own_in[c : c + 1]
                + scal(below, UPWARD) * u_ref[rows * c : rows * c + 1, :]
            )


def on_device(
    velocity,
    y_metric,
    forward_rate,
    backward_rate,
    pivot_inv,
    particle_vel,
    particle_cell,
    particle_offset,
    inverse_tau,
    outgoing_count,
):
    comps, cells_x, cells_y, cells_z = velocity.shape
    assert (comps, cells_x, cells_y) == (COMPS, 1, 16)
    slots = particle_vel.shape[1]
    size_x, size_y = lax.axis_size("gx"), lax.axis_size("gy")
    assert size_x % 2 == 0 and size_y % 2 == 0
    ring_x = [(i, (i + 1) % size_x) for i in range(size_x)]
    diagonal = [
        ((x + 1) % size_x * size_y + (y + 1) % size_y, x * size_y + y)
        for x in range(size_x)
        for y in range(size_y)
    ]
    same_pair = [(i, i ^ 1) for i in range(size_x)]
    next_pair = [(i, (i + (1 if i % 2 else -1)) % size_x) for i in range(size_x)]

    def both_sides(block):
        far = lax.ppermute(block, "gx", next_pair)
        return lax.ppermute(block, "gx", same_pair), far

    ring_y = [(i, (i + 1) % size_y) for i in range(size_y)]
    back_y = [(b, a) for a, b in ring_y]
    flip = lambda bits: [(i, i ^ bits) for i in range(size_y)]
    mixed = [(i, i ^ (4 if i % 2 else 2)) for i in range(size_y)]
    direct = size_y == 8

    u = velocity.reshape(COMPS * cells_y, cells_z)
    first = velocity[:, 0, 0, :]
    final = velocity[:, 0, cells_y - 1, :]
    planes = both_sides(u)
    yp = lax.ppermute(first, "gy", back_y)
    ym = lax.ppermute(final, "gy", ring_y)
    corner = lax.ppermute(first, ("gx", "gy"), diagonal)
    edges = (corner, corner)

    cell = particle_cell.reshape(1, slots)
    tau = inverse_tau.reshape(1, slots)
    like = lambda *shape: jax.ShapeDtypeStruct(shape, F32)
    matrix, answer, scal, live = call(
        tables_kernel,
        (like(SECTIONS, 56, 128), like(SECTIONS, cells_y, 128), like(SECTIONS, 2, 128),
         like(1, slots)),
        scalars(5),
        "tables",
    )(forward_rate, backward_rate, pivot_inv, y_metric, outgoing_count)
    v = particle_vel
    rows = COMPS * cells_y
    field_like, slots_like = like(rows, cells_z), like(COMPS, slots)
    for k in range(SECTIONS):
        last = k == SECTIONS - 1
        near = call(
            own_plane_kernel,
            slots_like,
            whole_in_vmem(3),
            "own_plane",
            [pltpu.VMEM((4 * rows, cells_z), BF16)],
        )(u, cell, particle_offset)
        sides = (u, ym, *planes, yp, *edges)
        out = call(
            functools.partial(section_kernel, k, TIME_STEP * SECTION_WEIGHTS[k], last),
            (field_like, like(16 if last else 8, cells_z), slots_like)
            + ((like(COMPS, CAP),) if last else ()),
            whole_in_vmem(len(sides) + 9),
            "section",
            [
                pltpu.VMEM((4 * (rows + 8), cells_z), BF16),
                pltpu.VMEM((2 * rows * (cells_z // DEPTH), slots), BF16),
                pltpu.VMEM((slots, DEPTH), BF16),
            ],
        )(*sides, cell, particle_offset, tau, live, v, near, matrix, answer, scal)
        w, pq, v = out[:3]
        if last:
            from_x = lax.ppermute(out[3], "gx", ring_x)
        if direct:
            partner = lax.ppermute(pq, "gy", flip(1))
            pair = jnp.stack([pq[:8], partner[:8]])
            side = lax.ppermute(pair, "gy", mixed)
            far = lax.ppermute(pair, "gy", flip(6))
            if last:
                side, from_x = lax.optimization_barrier((side, from_x))
            other = lax.ppermute(side, "gy", flip(1))
            gathered = (pq, partner, side, other, far)
            scratch = [pltpu.VMEM((size_y, 8, cells_z), F32)]
        else:
            gathered = (lax.all_gather(pq, "gy", axis=0),)
            scratch = []
        if last:
            more, shapes = (v, from_x), (field_like, slots_like)
        else:
            planes = both_sides(w)
            more, shapes = (), (field_like, like(8, cells_z), like(COMPS, cells_z))
        if k == 0:
            shapes = shapes + (like(size_y, 2, 128 * SECTIONS),)
        else:
            more = (known,) + more
        joined = call(
            functools.partial(join_kernel, k, last, size_y, direct),
            shapes,
            whole_in_vmem(len(gathered) + 2 + len(more)),
            "join",
            scratch,
        )(*gathered, w, answer, *more)
        if not last:
            u, yp, ym = joined[:3]
            if k == 0:
                known = joined[3]
            edges = both_sides(yp)
    u, moved = joined
    return (u.reshape(velocity.shape), moved)


def solution(mesh):
    return jax.shard_map(
        on_device,
        mesh=mesh,
        in_specs=(
            P(None, "gx", "gy", None),
            P("gy"),
            P(None, "gy"),
            P(None, "gy"),
            P(None, "gy"),
            P(None, ("gx", "gy")),
            P(("gx", "gy")),
            P(None, ("gx", "gy")),
            P(("gx", "gy")),
            P("gx", "gy", None),
        ),
        out_specs=(P(None, "gx", "gy", None), P(None, ("gx", "gy"))),
        check_vma=False,
    )
```

```python
import functools

import jax
import jax.numpy as jnp
from jax import lax
from jax.experimental import pallas as pl
from jax.experimental.pallas import tpu as pltpu
from jax.sharding import PartitionSpec as P

RESIDENT = 2048
CAP = 512
SECTIONS = 3

SECTION_WEIGHTS = (8.0 / 15.0, 5.0 / 12.0, 3.0 / 4.0)
TIME_STEP = 0.3
STREAM_SCALE = 2.0
SPAN_SCALE = 2.0
COUPLING = 0.5
COMPS = 3
TILE = 512
DEPTH = 256
VMEM_LIMIT = 32 * 1024 * 1024
ENTER, LEAVE, PIVOT, UPWARD, METRIC = range(16, 21)
ROW, COLUMN, INNER, GROUP, LIVE, EDGE = range(6)

F32 = jnp.float32
BF16 = jnp.bfloat16


def call(kernel, out_shape, in_specs, name, scratch_shapes=()):
    several = isinstance(out_shape, tuple)
    out_specs = whole_in_vmem(len(out_shape)) if several else whole_in_vmem(1)[0]
    return pl.pallas_call(
        kernel,
        out_shape=out_shape,
        in_specs=in_specs,
        out_specs=tuple(out_specs) if several else out_specs,
        scratch_shapes=scratch_shapes,
        compiler_params=pltpu.CompilerParams(vmem_limit_bytes=VMEM_LIMIT),
        name=name,
    )


def whole_in_vmem(count):
    return [pl.BlockSpec(memory_space=pltpu.VMEM)] * count


def scalars(count):
    return [pl.BlockSpec(memory_space=pltpu.SMEM)] * count


def across(row, depth):
    width = row.shape[1]
    shape = (DEPTH // 16, 16, width)
    order = lax.broadcasted_iota(jnp.int32, shape, 0) * 16 + lax.broadcasted_iota(jnp.int32, shape, 1)
    order = order.astype(F32).astype(BF16)
    one, none = jnp.ones((), BF16), jnp.zeros((), BF16)
    parts = []
    for k in range(depth // DEPTH):
        wanted = jnp.broadcast_to(row - float(DEPTH * k), (16, width)).astype(BF16)
        parts.append(jnp.where(order == wanted[None], one, none).reshape(DEPTH, width))
    return jnp.concatenate(parts, axis=0)


def down(row):
    width = row.shape[1]
    order = lax.broadcasted_iota(jnp.int32, (width, DEPTH), 1).astype(F32).astype(BF16)
    column = jnp.broadcast_to(row, (8, width)).T[:, 0:1]
    wanted = jnp.broadcast_to(column, (width, DEPTH)).astype(BF16)
    return jnp.where(order == wanted, jnp.ones((), BF16), jnp.zeros((), BF16))


def spread_out(values, group, groups):
    width = group.shape[1]
    shape = (groups // 16, 16, width)
    order = lax.broadcasted_iota(jnp.int32, shape, 0) * 16 + lax.broadcasted_iota(jnp.int32, shape, 1)
    order = order.astype(F32).astype(BF16)
    hit = order == jnp.broadcast_to(group, (16, width)).astype(BF16)[None]
    parts = []
    for value in values:
        value = jnp.broadcast_to(value, (16, width)).astype(BF16)[None]
        parts.append(jnp.where(hit, value, jnp.zeros((), BF16)).reshape(groups, width))
    return jnp.concatenate(parts, axis=0)


def split_rows(rows):
    length = rows.shape[1]
    high = rows.astype(BF16).astype(F32)
    low = rows - high
    ahead = [pltpu.roll(part, length - 1, 1) for part in (high, low)]
    return jnp.concatenate([high, low] + ahead, axis=0).astype(BF16)


def blend_z(values, fz):
    rows = values.shape[0] // 4
    near = values[:rows] + values[rows : 2 * rows]
    far = values[2 * rows : 3 * rows] + values[3 * rows :]
    return near * (1.0 - fz) + far * fz


def tables_kernel(
    cells_z,
    down_ref,
    up_ref,
    scale_ref,
    metric_ref,
    count_ref,
    cell_ref,
    off_ref,
    matrix_ref,
    answer_ref,
    scal_ref,
    slots_ref,
):
    slot = lax.broadcasted_iota(jnp.int32, cell_ref.shape, 1)
    remain = slot - RESIDENT
    heading = remain // CAP
    limit = jnp.where(
        heading <= 0,
        count_ref[0, 0, 0],
        jnp.where(heading == 1, count_ref[0, 0, 1], count_ref[0, 0, 2]),
    )
    sections, rows = down_ref.shape
    cell = cell_ref[...]
    row, place = cell // cells_z, cell % cells_z
    slots_ref[ROW : ROW + 1, :] = row.astype(F32)
    slots_ref[COLUMN : COLUMN + 1, :] = place.astype(F32)
    slots_ref[INNER : INNER + 1, :] = (place % DEPTH).astype(F32)
    slots_ref[GROUP : GROUP + 1, :] = (place // DEPTH * rows + row).astype(F32)
    slots_ref[LIVE : LIVE + 1, :] = jnp.where((remain < 0) | (remain % CAP < limit), 1.0, 0.0)
    slots_ref[EDGE : EDGE + 1, :] = jnp.where(row == rows - 1, off_ref[1:2, :], 0.0)
    lane = lax.broadcasted_iota(jnp.int32, (1, 128), 1)
    at = lambda place: jnp.where(lane == place, 1.0, 0.0)
    matrix_ref[...] = jnp.zeros_like(matrix_ref)
    scal_ref[...] = jnp.zeros_like(scal_ref)
    for k in range(sections):
        lower = []
        row = at(ENTER)
        for i in range(rows):
            row = down_ref[k, i] * row + at(i)
            lower.append(row)
        last = jnp.where(lane < rows, row, 0.0)
        for c in range(COMPS):
            place = COMPS * rows + c
            matrix_ref[k, place : place + 1, :] = pltpu.roll(last, rows * c, 1)
        scal_ref[k, 0:1, :] = row
        row = at(LEAVE)
        for i in reversed(range(rows)):
            row = scale_ref[k, i] * lower[i] + up_ref[k, i] * row
            inner = jnp.where(lane < rows, row, 0.0)
            for c in range(COMPS):
                place = rows * c + i
                matrix_ref[k, place : place + 1, :] = inner if c == 0 else pltpu.roll(inner, rows * c, 1)
            answer_ref[k, i : i + 1, :] = row + metric_ref[i] * at(METRIC)
        scal_ref[k, 1:2, :] = (
            row + scale_ref[k, rows - 1] * at(PIVOT) + up_ref[k, rows - 1] * at(UPWARD)
        )


def two_sides(one_ref, other_ref):
    even = lax.axis_index("gx") % 2 == 0
    one, other = one_ref[...], other_ref[...]
    return jnp.where(even, one, other), jnp.where(even, other, one)


def joined_plane(plane, ef, answer):
    enter, leave = answer[:, ENTER : ENTER + 1], answer[:, LEAVE : LEAVE + 1]
    rows = enter.shape[0]
    return jnp.concatenate(
        [
            plane[rows * c : rows * (c + 1)]
            + enter * ef[c : c + 1]
            + leave * ef[COMPS + c : COMPS + c + 1]
            for c in range(COMPS)
        ],
        axis=0,
    )


def pack(ef_ref, parts):
    for i, part in enumerate(parts):
        ef_ref[6 + i // 2 : 7 + i // 2, CAP * (i % 2) : CAP * (i % 2) + CAP] = part


def unpack(ef):
    return [ef[6 + i // 2 : 7 + i // 2, CAP * (i % 2) : CAP * (i % 2) + CAP] for i in range(4)]


def visitors_kernel(
    number,
    step,
    u_ref,
    ef_ref,
    near_x_ref,
    far_x_ref,
    near_ef_ref,
    far_ef_ref,
    near_old_ref,
    far_old_ref,
    answer_ref,
    out_ref,
):
    cells_z = u_ref.shape[1]
    rows = u_ref.shape[0] // COMPS
    count = COMPS * rows
    _, ef = two_sides(near_ef_ref, far_ef_ref)
    _, old = two_sides(near_old_ref, far_old_ref)
    _, plane = two_sides(near_x_ref, far_x_ref)
    plane = joined_plane(plane, ef, answer_ref[number - 1])
    pad = jnp.zeros((8 - COMPS, cells_z), F32)
    cell, fx, fy, fz = unpack(old)
    *v, tau = unpack(ef)
    row = jnp.floor(cell * (1.0 / cells_z))
    chosen = across(cell - row * cells_z, cells_z)
    behind = split_rows(jnp.concatenate([plane, ef[COMPS : 2 * COMPS], pad], axis=0))
    here = split_rows(jnp.concatenate([u_ref[...], ef_ref[COMPS : 2 * COMPS, :], pad], axis=0))
    blended = blend_z(jnp.dot(behind, chosen, preferred_element_type=F32), fz) * (1.0 - fx)
    blended = blended + blend_z(jnp.dot(here, chosen, preferred_element_type=F32), fz) * fx
    order = lax.broadcasted_iota(jnp.int32, (rows, CAP), 0).astype(F32)
    weight = jnp.where(order == row, 1.0 - fy, jnp.where(order == row + 1.0, fy, 0.0))
    edge = jnp.where(row == rows - 1.0, fy, 0.0)
    for c in range(COMPS):
        part = jnp.sum(blended[rows * c : rows * (c + 1)] * weight, axis=0, keepdims=True)
        fluid = part + blended[count + c : count + c + 1] * edge
        moved = v[c] + step * (tau * (fluid - v[c]))
        out_ref[c : c + 1, :] = jnp.where(cell >= 0.0, moved, 0.0)


def own_plane_kernel(u_ref, slots_ref, off_ref, out_ref, table_ref):
    cells_z = u_ref.shape[1]
    rows = u_ref.shape[0] // COMPS
    table_ref[...] = split_rows(u_ref[...])
    order = lax.broadcasted_iota(jnp.int32, (rows, TILE), 0).astype(F32)
    for t in range(slots_ref.shape[1] // TILE):
        here = slice(t * TILE, (t + 1) * TILE)
        row, column = (slots_ref[d : d + 1, here] for d in (ROW, COLUMN))
        fx, fy, fz = (off_ref[d : d + 1, here] for d in range(3))
        chosen = across(column, cells_z)
        blended = blend_z(jnp.dot(table_ref[...], chosen, preferred_element_type=F32), fz)
        weight = jnp.where(order == row, 1.0 - fy, jnp.where(order == row + 1.0, fy, 0.0))
        weight = weight * (1.0 - fx)
        for c in range(COMPS):
            part = blended[rows * c : rows * (c + 1)] * weight
            out_ref[c : c + 1, here] = jnp.sum(part, axis=0, keepdims=True)


def section_kernel(number, step, last, *refs):
    first = number == 0
    refs = list(refs)
    take = lambda count: [refs.pop(0) for _ in range(count)]
    u_ref, ym_ref, near_x_ref, far_x_ref, yp_ref, near_ef_ref, far_ef_ref = take(7)
    slots_ref, off_ref, tau_ref, v_ref, near_ref, matrix_ref, answer_ref, scal_ref = take(8)
    w_ref, pq_ref, v_out_ref = take(3)
    table_ref, spread_ref, chosen_ref = refs

    cells_z = u_ref.shape[1]
    rows = u_ref.shape[0] // COMPS
    count = COMPS * rows
    groups = rows * (cells_z // DEPTH)
    position = lax.axis_index("gy")
    top = jnp.where(position == lax.axis_size("gy") - 1, 0.0, 1.0).astype(F32)
    bottom = jnp.where(position == 0, 0.0, 1.0).astype(F32)
    x_plus, x_minus = two_sides(near_x_ref, far_x_ref)
    ahead, behind = two_sides(near_ef_ref, far_ef_ref)
    if first:
        chip, beside = yp_ref[...], ym_ref[...]
        below = position % 2 == 1
        y_plus = jnp.where(below, beside, chip)[:COMPS] * top
        y_minus = jnp.where(below, chip, beside)[COMPS:] * bottom
        corner = ahead * top
    else:
        y_minus = ym_ref[...] * bottom
        y_plus = yp_ref[COMPS : 2 * COMPS, :]
        corner = ahead[COMPS : 2 * COMPS]
        x_plus, x_minus = (
            joined_plane(plane, ef, answer_ref[number - 1])
            for plane, ef in ((x_plus, ahead), (x_minus, behind))
        )
    pad = jnp.zeros((2, cells_z), F32)
    table_ref[...] = split_rows(jnp.concatenate([x_plus, y_plus, corner, pad], axis=0))
    order = lax.broadcasted_iota(jnp.int32, (rows, TILE), 0).astype(F32)
    for t in range(slots_ref.shape[1] // TILE):
        here = slice(t * TILE, (t + 1) * TILE)
        row, column, inner, group, live, edge = (slots_ref[d : d + 1, here] for d in range(6))
        fx, fy, fz = (off_ref[d : d + 1, here] for d in range(3))
        found = jnp.dot(table_ref[...], across(column, cells_z), preferred_element_type=F32)
        chosen_ref[here, :] = down(inner)
        blended = blend_z(found, fz)
        weight = jnp.where(order == row, 1.0 - fy, jnp.where(order == row + 1.0, fy, 0.0)) * fx
        parts = [
            jnp.sum(blended[rows * c : rows * (c + 1)] * weight, axis=0, keepdims=True)
            for c in range(COMPS)
        ]
        side = blended[count : count + COMPS] * (1.0 - fx)
        side = side + blended[count + COMPS : count + 2 * COMPS] * fx
        fluid = near_ref[:, here] + jnp.concatenate(parts, axis=0) + side * edge
        v = v_ref[:, here]
        drag = tau_ref[:, here] * (fluid - v)
        v = v + step * drag
        v_out_ref[:, here] = v * live if last else v
        push = drag * live * (-COUPLING)
        high = push.astype(BF16).astype(F32)
        low = push - high
        pushes = [part[c : c + 1] for part in (high, low) for c in range(COMPS)]
        spread_ref[:, here] = spread_out(pushes, group, groups)
    pushed = jnp.dot(spread_ref[...], chosen_ref[...], preferred_element_type=F32)

    u = u_ref[...]
    slope_x = (x_plus - x_minus) * (0.5 * STREAM_SCALE)
    slope_z = (pltpu.roll(u, cells_z - 1, 1) - pltpu.roll(u, 1, 1)) * (0.5 * SPAN_SCALE)
    metric = 0.5 * answer_ref[number, :, METRIC : METRIC + 1]
    rhs = []
    for c in range(COMPS):
        own = slice(rows * c, rows * (c + 1))
        field = u[own]
        upper = jnp.concatenate([field[1:], y_plus[c : c + 1]], axis=0)
        lower = jnp.concatenate([y_minus[c : c + 1], field[:-1]], axis=0)
        slope_y = (upper - lower) * metric
        convection = -(
            u[:rows] * slope_x[own] + u[rows : 2 * rows] * slope_y + u[2 * rows :] * slope_z[own]
        )
        pieces = []
        for k in range(cells_z // DEPTH):
            high, low = (groups * (c + COMPS * i) + rows * k for i in range(2))
            pieces.append(pushed[high : high + rows] + pushed[low : low + rows])
        force = jnp.concatenate(pieces, axis=1)
        rhs.append(field + step * (convection + force))
    solved = jnp.dot(
        matrix_ref[number, :, 0:count],
        jnp.concatenate(rhs, axis=0),
        precision=lax.Precision.HIGHEST,
        preferred_element_type=F32,
    )
    w_ref[...] = solved[:count]
    pq_ref[0:COMPS, :] = solved[count : count + COMPS]
    for c in range(COMPS):
        pq_ref[COMPS + c : COMPS + c + 1, :] = solved[rows * c : rows * c + 1]
    pq_ref[6:, :] = jnp.zeros((pq_ref.shape[0] - 6, cells_z), F32)
    if first:
        for k in range(scal_ref.shape[0]):
            pq_ref[6:8, 128 * k : 128 * (k + 1)] = scal_ref[k]
    if last:
        lower = v_out_ref[:, RESIDENT + CAP : RESIDENT + 2 * CAP]
        upper = v_out_ref[:, RESIDENT + 2 * CAP :]
        even = position % 2 == 0
        for place, part in ((6, jnp.where(even, lower, upper)), (8, jnp.where(even, upper, lower))):
            pq_ref[place : place + 1, 0:CAP] = part[0:1]
            pq_ref[place : place + 1, CAP : 2 * CAP] = part[1:2]
            pq_ref[place + 1 : place + 2, 0:CAP] = part[2:3]


def join_kernel(number, last, blocks, direct, *refs):
    refs = list(refs)
    take = lambda count: [refs.pop(0) for _ in range(count)]
    here = lax.axis_index("gy")
    if direct:
        sources = take(5)
    else:
        (all_ref,) = take(1)
    w_ref, answer_ref = take(2)
    if number > 0:
        (known_ref,) = take(1)
    if last:
        v_ref, from_x_ref, u_ref, moved_ref = take(4)
    else:
        slots_ref, off_ref, tau_ref, v_ref = take(4)
        u_ref, ef_ref, ym_ref = take(3)
        if number == 0:
            (known_ref,) = take(1)
    if direct:
        (all_ref,) = refs
        own_ref, partner_ref, side_ref, other_ref, far_ref = sources
        odd = here % 2 == 1
        all_ref[here] = own_ref[0:8, :]
        all_ref[here ^ 1] = partner_ref[0:8, :]
        near = here ^ jnp.where(odd, 4, 2)
        all_ref[near] = side_ref[0]
        all_ref[near ^ 1] = side_ref[1]
        near = here ^ jnp.where(odd, 2, 4)
        all_ref[near ^ 1] = other_ref[0]
        all_ref[near] = other_ref[1]
        all_ref[here ^ 6] = far_ref[0]
        all_ref[here ^ 7] = far_ref[1]
    rows = w_ref.shape[0] // COMPS
    if number == 0:
        known_ref[...] = all_ref[:, 6:8, 0 : known_ref.shape[2]]

    def scal(k, which, row=1):
        place = 128 * number + which
        return known_ref[k, row : row + 1, place : place + 1]

    zero = jnp.zeros((COMPS, w_ref.shape[1]), F32)
    entering, own_in, at = zero, zero, []
    for k in range(blocks):
        at.append(entering)
        own_in = jnp.where(here == k, entering, own_in)
        entering = all_ref[k, 0:COMPS, :] + scal(k, ENTER, 0) * entering
    leaving, own_out = zero, zero
    for k in reversed(range(blocks)):
        own_out = jnp.where(here == k, leaving, own_out)
        leaving = (
            all_ref[k, COMPS : 2 * COMPS, :] + scal(k, ENTER) * at[k] + scal(k, LEAVE) * leaving
        )
    enter = answer_ref[number, :, ENTER : ENTER + 1]
    leave = answer_ref[number, :, LEAVE : LEAVE + 1]
    for c in range(COMPS):
        own = slice(rows * c, rows * (c + 1))
        u_ref[own, :] = w_ref[own, :] + enter * own_in[c : c + 1] + leave * own_out[c : c + 1]
    below = jnp.maximum(here - 1, 0)
    if last:
        even = here % 2 == 0
        keep_above = jnp.where(here == blocks - 1, 0.0, 1.0).astype(F32)
        keep_below = jnp.where(here == 0, 0.0, 1.0).astype(F32)
        across_chips = jnp.where(even, below, jnp.minimum(here + 1, blocks - 1))
        moved_ref[:, :RESIDENT] = v_ref[:, :RESIDENT]
        moved_ref[:, RESIDENT : RESIDENT + CAP] = from_x_ref[...]
        for c in range(COMPS):
            row, lanes = c // 2, slice(CAP * (c % 2), CAP * (c % 2) + CAP)
            beside = all_ref[across_chips, 6 + row : 7 + row, lanes]
            if direct:
                chip = partner_ref[8 + row : 9 + row, lanes]
            else:
                chip = all_ref[here ^ 1, 8 + row : 9 + row, lanes]
            own = slice(c, c + 1)
            moved_ref[own, RESIDENT + CAP : RESIDENT + 2 * CAP] = (
                jnp.where(even, chip, beside) * keep_above
            )
            moved_ref[own, RESIDENT + 2 * CAP :] = jnp.where(even, beside, chip) * keep_below
    else:
        ef_ref[0:COMPS, :] = own_in
        ef_ref[COMPS : 2 * COMPS, :] = own_out
        leaving = slice(RESIDENT, RESIDENT + CAP)
        if number == 0:
            cell = slots_ref[ROW : ROW + 1, leaving] * float(w_ref.shape[1])
            cell = cell + slots_ref[COLUMN : COLUMN + 1, leaving]
            cell = jnp.where(slots_ref[LIVE : LIVE + 1, leaving] > 0.0, cell, -1.0)
            pack(ef_ref, [cell] + [off_ref[d : d + 1, leaving] for d in range(3)])
        else:
            pack(ef_ref, [v_ref[c : c + 1, leaving] for c in range(COMPS)] + [tau_ref[:, leaving]])
        for c in range(COMPS):
            ym_ref[c : c + 1, :] = (
                scal(below, PIVOT) * own_in[c : c + 1]
                + scal(below, UPWARD) * u_ref[rows * c : rows * c + 1, :]
            )


def on_device(
    velocity,
    y_metric,
    forward_rate,
    backward_rate,
    pivot_inv,
    particle_vel,
    particle_cell,
    particle_offset,
    inverse_tau,
    outgoing_count,
):
    comps, cells_x, cells_y, cells_z = velocity.shape
    assert (comps, cells_x, cells_y) == (COMPS, 1, 16)
    assert cells_z == 2 * CAP and SECTIONS == 3
    slots = particle_vel.shape[1]
    size_x, size_y = lax.axis_size("gx"), lax.axis_size("gy")
    assert size_x % 2 == 0 and size_y % 2 == 0
    diagonal = [
        ((x + 1) % size_x * size_y + (y + 1) % size_y, x * size_y + y)
        for x in range(size_x)
        for y in range(size_y)
    ]
    same_pair = [(i, i ^ 1) for i in range(size_x)]
    next_pair = [(i, (i + (1 if i % 2 else -1)) % size_x) for i in range(size_x)]

    def both_sides(block):
        far = lax.ppermute(block, "gx", next_pair)
        return lax.ppermute(block, "gx", same_pair), far

    next_to = [(i, (i + (1 if i % 2 else -1)) % size_y) for i in range(size_y)]
    flip = lambda bits: [(i, i ^ bits) for i in range(size_y)]
    mixed = [(i, i ^ (4 if i % 2 else 2)) for i in range(size_y)]
    direct = size_y == 8

    u = velocity.reshape(COMPS * cells_y, cells_z)
    first = velocity[:, 0, 0, :]
    final = velocity[:, 0, cells_y - 1, :]
    planes = both_sides(u)
    corner = lax.ppermute(first, ("gx", "gy"), diagonal)
    both = jnp.concatenate([first, final], axis=0)
    ym = lax.ppermute(both, "gy", next_to)
    yp = lax.ppermute(both, "gy", flip(1))
    edges = (corner, corner)

    cell = particle_cell.reshape(1, slots)
    tau = inverse_tau.reshape(1, slots)
    like = lambda *shape: jax.ShapeDtypeStruct(shape, F32)
    matrix, answer, scal, places = call(
        functools.partial(tables_kernel, cells_z),
        (like(SECTIONS, 56, 128), like(SECTIONS, cells_y, 128), like(SECTIONS, 2, 128),
         like(8, slots)),
        scalars(5) + whole_in_vmem(2),
        "tables",
    )(forward_rate, backward_rate, pivot_inv, y_metric, outgoing_count, cell, particle_offset)
    v = particle_vel
    rows = COMPS * cells_y
    field_like, slots_like = like(rows, cells_z), like(COMPS, slots)
    for k in range(SECTIONS):
        last = k == SECTIONS - 1
        near = call(
            own_plane_kernel,
            slots_like,
            whole_in_vmem(3),
            "own_plane",
            [pltpu.VMEM((4 * rows, cells_z), BF16)],
        )(u, places, particle_offset)
        sides = (u, ym, *planes, yp, *edges)
        out = call(
            functools.partial(section_kernel, k, TIME_STEP * SECTION_WEIGHTS[k], last),
            (field_like, like(16 if last else 8, cells_z), slots_like),
            whole_in_vmem(len(sides) + 8),
            "section",
            [
                pltpu.VMEM((4 * (rows + 8), cells_z), BF16),
                pltpu.VMEM((2 * rows * (cells_z // DEPTH), slots), BF16),
                pltpu.VMEM((slots, DEPTH), BF16),
            ],
        )(*sides, places, particle_offset, tau, v, near, matrix, answer, scal)
        w, pq, v = out[:3]
        if last:
            from_x = call(
                functools.partial(visitors_kernel, k, TIME_STEP * SECTION_WEIGHTS[k]),
                like(COMPS, CAP),
                whole_in_vmem(9),
                "visitors",
            )(u, yp, *planes, *edges, *old_edges, answer)
        if direct:
            partner = lax.ppermute(pq, "gy", flip(1))
            if last:
                partner, from_x = lax.optimization_barrier((partner, from_x))
            pair = jnp.stack([pq[:8], partner[:8]])
            side = lax.ppermute(pair, "gy", mixed)
            far = lax.ppermute(pair, "gy", flip(6))
            other = lax.ppermute(side, "gy", flip(1))
            gathered = (pq, partner, side, other, far)
            scratch = [pltpu.VMEM((size_y, 8, cells_z), F32)]
        else:
            gathered = (lax.all_gather(pq, "gy", axis=0),)
            scratch = []
        if last:
            more, shapes = (v, from_x), (field_like, slots_like)
        else:
            planes = both_sides(w)
            more = (places, particle_offset, tau, v)
            shapes = (field_like, like(8, cells_z), like(COMPS, cells_z))
        if k == 0:
            shapes = shapes + (like(size_y, 2, 128 * SECTIONS),)
        else:
            more = (known,) + more
        joined = call(
            functools.partial(join_kernel, k, last, size_y, direct),
            shapes,
            whole_in_vmem(len(gathered) + 2 + len(more)),
            "join",
            scratch,
        )(*gathered, w, answer, *more)
        if not last:
            u, yp, ym = joined[:3]
            if k == 0:
                known = joined[3]
            old_edges, edges = edges, both_sides(yp)
    u, moved = joined
    return (u.reshape(velocity.shape), moved)


def solution(mesh):
    return jax.shard_map(
        on_device,
        mesh=mesh,
        in_specs=(
            P(None, "gx", "gy", None),
            P("gy"),
            P(None, "gy"),
            P(None, "gy"),
            P(None, "gy"),
            P(None, ("gx", "gy")),
            P(("gx", "gy")),
            P(None, ("gx", "gy")),
            P(("gx", "gy")),
            P("gx", "gy", None),
        ),
        out_specs=(P(None, "gx", "gy", None), P(None, ("gx", "gy"))),
        check_vma=False,
    )
```

```python
import functools

import jax
import jax.numpy as jnp
from jax import lax
from jax.experimental import pallas as pl
from jax.experimental.pallas import tpu as pltpu
from jax.sharding import PartitionSpec as P

RESIDENT = 2048
CAP = 512
SECTIONS = 3

SECTION_WEIGHTS = (8.0 / 15.0, 5.0 / 12.0, 3.0 / 4.0)
TIME_STEP = 0.3
STREAM_SCALE = 2.0
SPAN_SCALE = 2.0
COUPLING = 0.5
COMPS = 3
TILE = 512
DEPTH = 256
VMEM_LIMIT = 32 * 1024 * 1024
ENTER, LEAVE, PIVOT, UPWARD, METRIC = range(16, 21)
ROW, COLUMN, INNER, GROUP, LIVE, EDGE, SHARES = range(7)

F32 = jnp.float32
BF16 = jnp.bfloat16


def call(kernel, out_shape, in_specs, name, scratch_shapes=()):
    several = isinstance(out_shape, tuple)
    out_specs = whole_in_vmem(len(out_shape)) if several else whole_in_vmem(1)[0]
    return pl.pallas_call(
        kernel,
        out_shape=out_shape,
        in_specs=in_specs,
        out_specs=tuple(out_specs) if several else out_specs,
        scratch_shapes=scratch_shapes,
        compiler_params=pltpu.CompilerParams(vmem_limit_bytes=VMEM_LIMIT),
        name=name,
    )


def whole_in_vmem(count):
    return [pl.BlockSpec(memory_space=pltpu.VMEM)] * count


def scalars(count):
    return [pl.BlockSpec(memory_space=pltpu.SMEM)] * count


def across(row, depth):
    width = row.shape[1]
    shape = (DEPTH // 16, 16, width)
    order = lax.broadcasted_iota(jnp.int32, shape, 0) * 16 + lax.broadcasted_iota(jnp.int32, shape, 1)
    order = order.astype(F32).astype(BF16)
    one, none = jnp.ones((), BF16), jnp.zeros((), BF16)
    parts = []
    for k in range(depth // DEPTH):
        wanted = jnp.broadcast_to(row - float(DEPTH * k), (16, width)).astype(BF16)
        parts.append(jnp.where(order == wanted[None], one, none).reshape(DEPTH, width))
    return jnp.concatenate(parts, axis=0)


def down(row):
    width = row.shape[1]
    order = lax.broadcasted_iota(jnp.int32, (width, DEPTH), 1).astype(F32).astype(BF16)
    column = jnp.broadcast_to(row, (8, width)).T[:, 0:1]
    wanted = jnp.broadcast_to(column, (width, DEPTH)).astype(BF16)
    return jnp.where(order == wanted, jnp.ones((), BF16), jnp.zeros((), BF16))


def spread_out(values, group, groups):
    width = group.shape[1]
    shape = (groups // 16, 16, width)
    order = lax.broadcasted_iota(jnp.int32, shape, 0) * 16 + lax.broadcasted_iota(jnp.int32, shape, 1)
    order = order.astype(F32).astype(BF16)
    hit = order == jnp.broadcast_to(group, (16, width)).astype(BF16)[None]
    parts = []
    for value in values:
        value = jnp.broadcast_to(value, (16, width)).astype(BF16)[None]
        parts.append(jnp.where(hit, value, jnp.zeros((), BF16)).reshape(groups, width))
    return jnp.concatenate(parts, axis=0)


def split_rows(rows):
    length = rows.shape[1]
    high = rows.astype(BF16).astype(F32)
    low = rows - high
    ahead = [pltpu.roll(part, length - 1, 1) for part in (high, low)]
    return jnp.concatenate([high, low] + ahead, axis=0).astype(BF16)


def blend_z(values, fz):
    rows = values.shape[0] // 4
    near = values[:rows] + values[rows : 2 * rows]
    far = values[2 * rows : 3 * rows] + values[3 * rows :]
    return near * (1.0 - fz) + far * fz


def tables_kernel(
    cells_z,
    down_ref,
    up_ref,
    scale_ref,
    metric_ref,
    count_ref,
    cell_ref,
    off_ref,
    matrix_ref,
    answer_ref,
    scal_ref,
    slots_ref,
):
    slot = lax.broadcasted_iota(jnp.int32, cell_ref.shape, 1)
    remain = slot - RESIDENT
    heading = remain // CAP
    limit = jnp.where(
        heading <= 0,
        count_ref[0, 0, 0],
        jnp.where(heading == 1, count_ref[0, 0, 1], count_ref[0, 0, 2]),
    )
    sections, rows = down_ref.shape
    cell = cell_ref[...]
    row, place = cell // cells_z, cell % cells_z
    slots_ref[...] = jnp.zeros_like(slots_ref)
    slots_ref[ROW : ROW + 1, :] = row.astype(F32)
    slots_ref[COLUMN : COLUMN + 1, :] = place.astype(F32)
    slots_ref[INNER : INNER + 1, :] = (place % DEPTH).astype(F32)
    slots_ref[GROUP : GROUP + 1, :] = (place // DEPTH * rows + row).astype(F32)
    slots_ref[LIVE : LIVE + 1, :] = jnp.where((remain < 0) | (remain % CAP < limit), 1.0, 0.0)
    slots_ref[EDGE : EDGE + 1, :] = jnp.where(row == rows - 1, off_ref[1:2, :], 0.0)
    lane = lax.broadcasted_iota(jnp.int32, (1, 128), 1)
    at = lambda place: jnp.where(lane == place, 1.0, 0.0)
    matrix_ref[...] = jnp.zeros_like(matrix_ref)
    scal_ref[...] = jnp.zeros_like(scal_ref)
    order = lax.broadcasted_iota(jnp.int32, (rows, 1), 0)
    fy = off_ref[1:2, :]
    weight = jnp.where(order == row, 1.0 - fy, jnp.where(order == row + 1, fy, 0.0))
    edge = slots_ref[EDGE : EDGE + 1, :]
    for k in range(sections):
        lower = []
        row = at(ENTER)
        for i in range(rows):
            row = down_ref[k, i] * row + at(i)
            lower.append(row)
        last = jnp.where(lane < rows, row, 0.0)
        for c in range(COMPS):
            place = COMPS * rows + c
            matrix_ref[k, place : place + 1, :] = pltpu.roll(last, rows * c, 1)
        scal_ref[k, 0:1, :] = row
        row = at(LEAVE)
        for i in reversed(range(rows)):
            row = scale_ref[k, i] * lower[i] + up_ref[k, i] * row
            inner = jnp.where(lane < rows, row, 0.0)
            for c in range(COMPS):
                place = rows * c + i
                matrix_ref[k, place : place + 1, :] = inner if c == 0 else pltpu.roll(inner, rows * c, 1)
            answer_ref[k, i : i + 1, :] = row + metric_ref[i] * at(METRIC)
        if k < sections - 1:
            for i, which, more in ((0, ENTER, 0.0), (1, LEAVE, edge)):
                share = jnp.sum(
                    weight * answer_ref[k, :, which : which + 1], axis=0, keepdims=True
                )
                place = SHARES + 2 * k + i
                slots_ref[place : place + 1, :] = share + more
        scal_ref[k, 1:2, :] = (
            row + scale_ref[k, rows - 1] * at(PIVOT) + up_ref[k, rows - 1] * at(UPWARD)
        )


def two_sides(one_ref, other_ref):
    even = lax.axis_index("gx") % 2 == 0
    one, other = one_ref[...], other_ref[...]
    return jnp.where(even, one, other), jnp.where(even, other, one)


def joined_plane(plane, ef, answer):
    enter, leave = answer[:, ENTER : ENTER + 1], answer[:, LEAVE : LEAVE + 1]
    rows = enter.shape[0]
    return jnp.concatenate(
        [
            plane[rows * c : rows * (c + 1)]
            + enter * ef[c : c + 1]
            + leave * ef[COMPS + c : COMPS + c + 1]
            for c in range(COMPS)
        ],
        axis=0,
    )


def pack(ef_ref, parts):
    for i, part in enumerate(parts):
        ef_ref[6 + i // 2 : 7 + i // 2, CAP * (i % 2) : CAP * (i % 2) + CAP] = part


def unpack(ef):
    return [ef[6 + i // 2 : 7 + i // 2, CAP * (i % 2) : CAP * (i % 2) + CAP] for i in range(4)]


def visitors_kernel(
    number,
    step,
    u_ref,
    ef_ref,
    near_x_ref,
    far_x_ref,
    near_ef_ref,
    far_ef_ref,
    near_old_ref,
    far_old_ref,
    answer_ref,
    out_ref,
):
    cells_z = u_ref.shape[1]
    rows = u_ref.shape[0] // COMPS
    count = COMPS * rows
    _, ef = two_sides(near_ef_ref, far_ef_ref)
    _, old = two_sides(near_old_ref, far_old_ref)
    _, plane = two_sides(near_x_ref, far_x_ref)
    plane = joined_plane(plane, ef, answer_ref[number - 1])
    pad = jnp.zeros((8 - COMPS, cells_z), F32)
    cell, fx, fy, fz = unpack(old)
    *v, tau = unpack(ef)
    row = jnp.floor(cell * (1.0 / cells_z))
    chosen = across(cell - row * cells_z, cells_z)
    behind = split_rows(jnp.concatenate([plane, ef[COMPS : 2 * COMPS], pad], axis=0))
    here = split_rows(jnp.concatenate([u_ref[...], ef_ref[COMPS : 2 * COMPS, :], pad], axis=0))
    blended = blend_z(jnp.dot(behind, chosen, preferred_element_type=F32), fz) * (1.0 - fx)
    blended = blended + blend_z(jnp.dot(here, chosen, preferred_element_type=F32), fz) * fx
    order = lax.broadcasted_iota(jnp.int32, (rows, CAP), 0).astype(F32)
    weight = jnp.where(order == row, 1.0 - fy, jnp.where(order == row + 1.0, fy, 0.0))
    edge = jnp.where(row == rows - 1.0, fy, 0.0)
    for c in range(COMPS):
        part = jnp.sum(blended[rows * c : rows * (c + 1)] * weight, axis=0, keepdims=True)
        fluid = part + blended[count + c : count + c + 1] * edge
        moved = v[c] + step * (tau * (fluid - v[c]))
        out_ref[c : c + 1, :] = jnp.where(cell >= 0.0, moved, 0.0)


def own_plane_kernel(u_ref, slots_ref, off_ref, out_ref, table_ref):
    cells_z = u_ref.shape[1]
    rows = u_ref.shape[0] // COMPS
    table_ref[...] = split_rows(u_ref[...])
    order = lax.broadcasted_iota(jnp.int32, (rows, TILE), 0).astype(F32)
    for t in range(slots_ref.shape[1] // TILE):
        here = slice(t * TILE, (t + 1) * TILE)
        row, column = (slots_ref[d : d + 1, here] for d in (ROW, COLUMN))
        fx, fy, fz = (off_ref[d : d + 1, here] for d in range(3))
        chosen = across(column, cells_z)
        blended = blend_z(jnp.dot(table_ref[...], chosen, preferred_element_type=F32), fz)
        weight = jnp.where(order == row, 1.0 - fy, jnp.where(order == row + 1.0, fy, 0.0))
        weight = weight * (1.0 - fx)
        for c in range(COMPS):
            part = blended[rows * c : rows * (c + 1)] * weight
            out_ref[c : c + 1, here] = jnp.sum(part, axis=0, keepdims=True)


def ahead_plane_kernel(near_x_ref, far_x_ref, slots_ref, off_ref, own_ref, out_ref, table_ref):
    plane, _ = two_sides(near_x_ref, far_x_ref)
    cells_z = plane.shape[1]
    rows = plane.shape[0] // COMPS
    table_ref[...] = split_rows(plane)
    order = lax.broadcasted_iota(jnp.int32, (rows, TILE), 0).astype(F32)
    for t in range(slots_ref.shape[1] // TILE):
        here = slice(t * TILE, (t + 1) * TILE)
        row, column = (slots_ref[d : d + 1, here] for d in (ROW, COLUMN))
        fx, fy, fz = (off_ref[d : d + 1, here] for d in range(3))
        chosen = across(column, cells_z)
        blended = blend_z(jnp.dot(table_ref[...], chosen, preferred_element_type=F32), fz)
        weight = jnp.where(order == row, 1.0 - fy, jnp.where(order == row + 1.0, fy, 0.0)) * fx
        for c in range(COMPS):
            part = blended[rows * c : rows * (c + 1)] * weight
            part = jnp.sum(part, axis=0, keepdims=True)
            out_ref[c : c + 1, here] = own_ref[c : c + 1, here] + part


def section_kernel(number, step, last, *refs):
    first = number == 0
    refs = list(refs)
    take = lambda count: [refs.pop(0) for _ in range(count)]
    u_ref, ym_ref, near_x_ref, far_x_ref, yp_ref, near_ef_ref, far_ef_ref = take(7)
    slots_ref, off_ref, tau_ref, v_ref, near_ref, matrix_ref, answer_ref, scal_ref = take(8)
    w_ref, pq_ref, v_out_ref = take(3)
    table_ref, spread_ref, chosen_ref = refs

    cells_z = u_ref.shape[1]
    rows = u_ref.shape[0] // COMPS
    count = COMPS * rows
    groups = rows * (cells_z // DEPTH)
    position = lax.axis_index("gy")
    top = jnp.where(position == lax.axis_size("gy") - 1, 0.0, 1.0).astype(F32)
    bottom = jnp.where(position == 0, 0.0, 1.0).astype(F32)
    x_plus, x_minus = two_sides(near_x_ref, far_x_ref)
    ahead, behind = two_sides(near_ef_ref, far_ef_ref)
    if first:
        chip, beside = yp_ref[...], ym_ref[...]
        below = position % 2 == 1
        y_plus = jnp.where(below, beside, chip)[:COMPS] * top
        y_minus = jnp.where(below, chip, beside)[COMPS:] * bottom
        corner = ahead * top
    else:
        y_minus = ym_ref[...] * bottom
        y_plus = yp_ref[COMPS : 2 * COMPS, :]
        corner = ahead[COMPS : 2 * COMPS]
        x_plus, x_minus = (
            joined_plane(plane, ef, answer_ref[number - 1])
            for plane, ef in ((x_plus, ahead), (x_minus, behind))
        )
    if first:
        edge_rows = [
            jnp.concatenate(
                [jnp.zeros((COMPS, cells_z), F32), row, jnp.zeros((2, cells_z), F32)], axis=0
            )
            for row in (y_plus, corner)
        ]
    else:
        edge_rows = [yp_ref[...], ahead]
    table = split_rows(jnp.concatenate(edge_rows, axis=0))
    tall = table.shape[0]
    for k in range(cells_z // DEPTH):
        table_ref[tall * k : tall * (k + 1), :] = table[:, DEPTH * k : DEPTH * (k + 1)]
    upper_half = lax.broadcasted_iota(jnp.int32, (8, TILE), 0) >= COMPS
    for t in range(slots_ref.shape[1] // TILE):
        here = slice(t * TILE, (t + 1) * TILE)
        column, inner, group, live, edge = (
            slots_ref[d : d + 1, here] for d in (COLUMN, INNER, GROUP, LIVE, EDGE)
        )
        fx, fz = off_ref[0:1, here], off_ref[2:3, here]
        chosen_ref[here, :] = down(inner)
        found = jnp.dot(table_ref[...], across(inner, DEPTH), preferred_element_type=F32)
        picked = found[:tall]
        for k in range(1, cells_z // DEPTH):
            picked = jnp.where(column >= float(DEPTH * k), found[tall * k : tall * (k + 1)], picked)
        blended = blend_z(picked, fz)
        if first:
            enters, leaves = 0.0, edge
        else:
            enters, leaves = (
                slots_ref[d : d + 1, here]
                for d in (SHARES + 2 * (number - 1), SHARES + 2 * (number - 1) + 1)
            )
        more = blended[:8] * (1.0 - fx) + blended[8:] * fx
        more = more * jnp.where(upper_half, leaves, enters)
        fluid = near_ref[:, here] + more[:COMPS] + more[COMPS : 2 * COMPS]
        v = v_ref[:, here]
        drag = tau_ref[:, here] * (fluid - v)
        v = v + step * drag
        v_out_ref[:, here] = v * live if last else v
        push = drag * live * (-COUPLING)
        high = push.astype(BF16).astype(F32)
        low = push - high
        pushes = [part[c : c + 1] for part in (high, low) for c in range(COMPS)]
        spread_ref[:, here] = spread_out(pushes, group, groups)
    pushed = jnp.dot(spread_ref[...], chosen_ref[...], preferred_element_type=F32)

    u = u_ref[...]
    slope_x = (x_plus - x_minus) * (0.5 * STREAM_SCALE)
    slope_z = (pltpu.roll(u, cells_z - 1, 1) - pltpu.roll(u, 1, 1)) * (0.5 * SPAN_SCALE)
    metric = 0.5 * answer_ref[number, :, METRIC : METRIC + 1]
    rhs = []
    for c in range(COMPS):
        own = slice(rows * c, rows * (c + 1))
        field = u[own]
        upper = jnp.concatenate([field[1:], y_plus[c : c + 1]], axis=0)
        lower = jnp.concatenate([y_minus[c : c + 1], field[:-1]], axis=0)
        slope_y = (upper - lower) * metric
        convection = -(
            u[:rows] * slope_x[own] + u[rows : 2 * rows] * slope_y + u[2 * rows :] * slope_z[own]
        )
        pieces = []
        for k in range(cells_z // DEPTH):
            high, low = (groups * (c + COMPS * i) + rows * k for i in range(2))
            pieces.append(pushed[high : high + rows] + pushed[low : low + rows])
        force = jnp.concatenate(pieces, axis=1)
        rhs.append(field + step * (convection + force))
    solved = jnp.dot(
        matrix_ref[number, :, 0:count],
        jnp.concatenate(rhs, axis=0),
        precision=lax.Precision.HIGHEST,
        preferred_element_type=F32,
    )
    w_ref[...] = solved[:count]
    pq_ref[0:COMPS, :] = solved[count : count + COMPS]
    for c in range(COMPS):
        pq_ref[COMPS + c : COMPS + c + 1, :] = solved[rows * c : rows * c + 1]
    pq_ref[6:, :] = jnp.zeros((pq_ref.shape[0] - 6, cells_z), F32)
    if first:
        for k in range(scal_ref.shape[0]):
            pq_ref[6:8, 128 * k : 128 * (k + 1)] = scal_ref[k]
    if last:
        lower = v_out_ref[:, RESIDENT + CAP : RESIDENT + 2 * CAP]
        upper = v_out_ref[:, RESIDENT + 2 * CAP :]
        even = position % 2 == 0
        for place, part in ((6, jnp.where(even, lower, upper)), (8, jnp.where(even, upper, lower))):
            pq_ref[place : place + 1, 0:CAP] = part[0:1]
            pq_ref[place : place + 1, CAP : 2 * CAP] = part[1:2]
            pq_ref[place + 1 : place + 2, 0:CAP] = part[2:3]


def join_kernel(number, last, blocks, direct, *refs):
    refs = list(refs)
    take = lambda count: [refs.pop(0) for _ in range(count)]
    here = lax.axis_index("gy")
    if direct:
        sources = take(5)
    else:
        (all_ref,) = take(1)
    w_ref, answer_ref = take(2)
    if number > 0:
        (known_ref,) = take(1)
    if last:
        v_ref, from_x_ref, u_ref, moved_ref = take(4)
    else:
        slots_ref, off_ref, tau_ref, v_ref = take(4)
        u_ref, ef_ref, ym_ref = take(3)
        if number == 0:
            (known_ref,) = take(1)
    if direct:
        (all_ref,) = refs
        own_ref, partner_ref, side_ref, other_ref, far_ref = sources
        odd = here % 2 == 1
        all_ref[here] = own_ref[0:8, :]
        all_ref[here ^ 1] = partner_ref[0:8, :]
        near = here ^ jnp.where(odd, 4, 2)
        all_ref[near] = side_ref[0]
        all_ref[near ^ 1] = side_ref[1]
        near = here ^ jnp.where(odd, 2, 4)
        all_ref[near ^ 1] = other_ref[0]
        all_ref[near] = other_ref[1]
        all_ref[here ^ 6] = far_ref[0]
        all_ref[here ^ 7] = far_ref[1]
    rows = w_ref.shape[0] // COMPS
    if number == 0:
        known_ref[...] = all_ref[:, 6:8, 0 : known_ref.shape[2]]

    def scal(k, which, row=1):
        place = 128 * number + which
        return known_ref[k, row : row + 1, place : place + 1]

    zero = jnp.zeros((COMPS, w_ref.shape[1]), F32)
    entering, own_in, at = zero, zero, []
    for k in range(blocks):
        at.append(entering)
        own_in = jnp.where(here == k, entering, own_in)
        entering = all_ref[k, 0:COMPS, :] + scal(k, ENTER, 0) * entering
    leaving, own_out = zero, zero
    for k in reversed(range(blocks)):
        own_out = jnp.where(here == k, leaving, own_out)
        leaving = (
            all_ref[k, COMPS : 2 * COMPS, :] + scal(k, ENTER) * at[k] + scal(k, LEAVE) * leaving
        )
    enter = answer_ref[number, :, ENTER : ENTER + 1]
    leave = answer_ref[number, :, LEAVE : LEAVE + 1]
    for c in range(COMPS):
        own = slice(rows * c, rows * (c + 1))
        u_ref[own, :] = w_ref[own, :] + enter * own_in[c : c + 1] + leave * own_out[c : c + 1]
    below = jnp.maximum(here - 1, 0)
    if last:
        even = here % 2 == 0
        keep_above = jnp.where(here == blocks - 1, 0.0, 1.0).astype(F32)
        keep_below = jnp.where(here == 0, 0.0, 1.0).astype(F32)
        across_chips = jnp.where(even, below, jnp.minimum(here + 1, blocks - 1))
        moved_ref[:, :RESIDENT] = v_ref[:, :RESIDENT]
        moved_ref[:, RESIDENT : RESIDENT + CAP] = from_x_ref[...]
        for c in range(COMPS):
            row, lanes = c // 2, slice(CAP * (c % 2), CAP * (c % 2) + CAP)
            beside = all_ref[across_chips, 6 + row : 7 + row, lanes]
            if direct:
                chip = partner_ref[8 + row : 9 + row, lanes]
            else:
                chip = all_ref[here ^ 1, 8 + row : 9 + row, lanes]
            own = slice(c, c + 1)
            moved_ref[own, RESIDENT + CAP : RESIDENT + 2 * CAP] = (
                jnp.where(even, chip, beside) * keep_above
            )
            moved_ref[own, RESIDENT + 2 * CAP :] = jnp.where(even, beside, chip) * keep_below
    else:
        ef_ref[0:COMPS, :] = own_in
        ef_ref[COMPS : 2 * COMPS, :] = own_out
        leaving = slice(RESIDENT, RESIDENT + CAP)
        if number == 0:
            cell = slots_ref[ROW : ROW + 1, leaving] * float(w_ref.shape[1])
            cell = cell + slots_ref[COLUMN : COLUMN + 1, leaving]
            cell = jnp.where(slots_ref[LIVE : LIVE + 1, leaving] > 0.0, cell, -1.0)
            pack(ef_ref, [cell] + [off_ref[d : d + 1, leaving] for d in range(3)])
        else:
            pack(ef_ref, [v_ref[c : c + 1, leaving] for c in range(COMPS)] + [tau_ref[:, leaving]])
        for c in range(COMPS):
            ym_ref[c : c + 1, :] = (
                scal(below, PIVOT) * own_in[c : c + 1]
                + scal(below, UPWARD) * u_ref[rows * c : rows * c + 1, :]
            )


def on_device(
    velocity,
    y_metric,
    forward_rate,
    backward_rate,
    pivot_inv,
    particle_vel,
    particle_cell,
    particle_offset,
    inverse_tau,
    outgoing_count,
):
    comps, cells_x, cells_y, cells_z = velocity.shape
    assert (comps, cells_x, cells_y) == (COMPS, 1, 16)
    assert cells_z == 2 * CAP and SECTIONS == 3
    slots = particle_vel.shape[1]
    size_x, size_y = lax.axis_size("gx"), lax.axis_size("gy")
    assert size_x % 2 == 0 and size_y % 2 == 0
    diagonal = [
        ((x + 1) % size_x * size_y + (y + 1) % size_y, x * size_y + y)
        for x in range(size_x)
        for y in range(size_y)
    ]
    same_pair = [(i, i ^ 1) for i in range(size_x)]
    next_pair = [(i, (i + (1 if i % 2 else -1)) % size_x) for i in range(size_x)]

    def both_sides(block):
        far = lax.ppermute(block, "gx", next_pair)
        return lax.ppermute(block, "gx", same_pair), far

    next_to = [(i, (i + (1 if i % 2 else -1)) % size_y) for i in range(size_y)]
    flip = lambda bits: [(i, i ^ bits) for i in range(size_y)]
    mixed = [(i, i ^ (4 if i % 2 else 2)) for i in range(size_y)]
    direct = size_y == 8

    u = velocity.reshape(COMPS * cells_y, cells_z)
    first = velocity[:, 0, 0, :]
    final = velocity[:, 0, cells_y - 1, :]
    planes = both_sides(u)
    corner = lax.ppermute(first, ("gx", "gy"), diagonal)
    both = jnp.concatenate([first, final], axis=0)
    ym = lax.ppermute(both, "gy", next_to)
    yp = lax.ppermute(both, "gy", flip(1))
    edges = (corner, corner)

    cell = particle_cell.reshape(1, slots)
    tau = inverse_tau.reshape(1, slots)
    like = lambda *shape: jax.ShapeDtypeStruct(shape, F32)
    matrix, answer, scal, places = call(
        functools.partial(tables_kernel, cells_z),
        (like(SECTIONS, 56, 128), like(SECTIONS, cells_y, 128), like(SECTIONS, 2, 128),
         like(16, slots)),
        scalars(5) + whole_in_vmem(2),
        "tables",
    )(forward_rate, backward_rate, pivot_inv, y_metric, outgoing_count, cell, particle_offset)
    v = particle_vel
    rows = COMPS * cells_y
    field_like, slots_like = like(rows, cells_z), like(COMPS, slots)

    def own_plane(plane):
        return call(
            own_plane_kernel,
            slots_like,
            whole_in_vmem(3),
            "own_plane",
            [pltpu.VMEM((4 * rows, cells_z), BF16)],
        )(plane, places, particle_offset)

    own_near = own_plane(u)
    for k in range(SECTIONS):
        last = k == SECTIONS - 1
        near = call(
            ahead_plane_kernel,
            slots_like,
            whole_in_vmem(5),
            "ahead_plane",
            [pltpu.VMEM((4 * rows, cells_z), BF16)],
        )(*planes, places, particle_offset, own_near)
        sides = (u, ym, *planes, yp, *edges)
        out = call(
            functools.partial(section_kernel, k, TIME_STEP * SECTION_WEIGHTS[k], last),
            (field_like, like(16 if last else 8, cells_z), slots_like),
            whole_in_vmem(len(sides) + 8),
            "section",
            [
                pltpu.VMEM((4 * 16 * cells_z // DEPTH, DEPTH), BF16),
                pltpu.VMEM((2 * rows * (cells_z // DEPTH), slots), BF16),
                pltpu.VMEM((slots, DEPTH), BF16),
            ],
        )(*sides, places, particle_offset, tau, v, near, matrix, answer, scal)
        w, pq, v = out[:3]
        if last:
            from_x = call(
                functools.partial(visitors_kernel, k, TIME_STEP * SECTION_WEIGHTS[k]),
                like(COMPS, CAP),
                whole_in_vmem(9),
                "visitors",
            )(u, yp, *planes, *edges, *old_edges, answer)
        if direct:
            partner = lax.ppermute(pq, "gy", flip(1))
            if last:
                partner, from_x = lax.optimization_barrier((partner, from_x))
            pair = jnp.stack([pq[:8], partner[:8]])
            side = lax.ppermute(pair, "gy", mixed)
            far = lax.ppermute(pair, "gy", flip(6))
            other = lax.ppermute(side, "gy", flip(1))
            gathered = (pq, partner, side, other, far)
            scratch = [pltpu.VMEM((size_y, 8, cells_z), F32)]
        else:
            gathered = (lax.all_gather(pq, "gy", axis=0),)
            scratch = []
        if last:
            more, shapes = (v, from_x), (field_like, slots_like)
        else:
            planes = both_sides(w)
            own_near = own_plane(w)
            more = (places, particle_offset, tau, v)
            shapes = (field_like, like(8, cells_z), like(COMPS, cells_z))
        if k == 0:
            shapes = shapes + (like(size_y, 2, 128 * SECTIONS),)
        else:
            more = (known,) + more
        joined = call(
            functools.partial(join_kernel, k, last, size_y, direct),
            shapes,
            whole_in_vmem(len(gathered) + 2 + len(more)),
            "join",
            scratch,
        )(*gathered, w, answer, *more)
        if not last:
            u, yp, ym = joined[:3]
            if k == 0:
                known = joined[3]
            old_edges, edges = edges, both_sides(yp)
    u, moved = joined
    return (u.reshape(velocity.shape), moved)


def solution(mesh):
    return jax.shard_map(
        on_device,
        mesh=mesh,
        in_specs=(
            P(None, "gx", "gy", None),
            P("gy"),
            P(None, "gy"),
            P(None, "gy"),
            P(None, "gy"),
            P(None, ("gx", "gy")),
            P(("gx", "gy")),
            P(None, ("gx", "gy")),
            P(("gx", "gy")),
            P("gx", "gy", None),
        ),
        out_specs=(P(None, "gx", "gy", None), P(None, ("gx", "gy"))),
        check_vma=False,
    )
```

```python
import functools

import jax
import jax.numpy as jnp
from jax import lax
from jax.experimental import pallas as pl
from jax.experimental.pallas import tpu as pltpu
from jax.sharding import PartitionSpec as P

RESIDENT = 2048
CAP = 512
SECTIONS = 3

SECTION_WEIGHTS = (8.0 / 15.0, 5.0 / 12.0, 3.0 / 4.0)
TIME_STEP = 0.3
STREAM_SCALE = 2.0
SPAN_SCALE = 2.0
COUPLING = 0.5
COMPS = 3
TILE = 512
DEPTH = 256
VMEM_LIMIT = 32 * 1024 * 1024
ENTER, LEAVE, PIVOT, UPWARD, METRIC = range(16, 21)
ROW, COLUMN, INNER, GROUP, LIVE, EDGE, SHARES = range(7)

F32 = jnp.float32
BF16 = jnp.bfloat16


def call(kernel, out_shape, in_specs, name, scratch_shapes=()):
    several = isinstance(out_shape, tuple)
    out_specs = whole_in_vmem(len(out_shape)) if several else whole_in_vmem(1)[0]
    return pl.pallas_call(
        kernel,
        out_shape=out_shape,
        in_specs=in_specs,
        out_specs=tuple(out_specs) if several else out_specs,
        scratch_shapes=scratch_shapes,
        compiler_params=pltpu.CompilerParams(vmem_limit_bytes=VMEM_LIMIT),
        name=name,
    )


def whole_in_vmem(count):
    return [pl.BlockSpec(memory_space=pltpu.VMEM)] * count


def scalars(count):
    return [pl.BlockSpec(memory_space=pltpu.SMEM)] * count


def across(row, depth):
    width = row.shape[1]
    shape = (DEPTH // 16, 16, width)
    order = lax.broadcasted_iota(jnp.int32, shape, 0) * 16 + lax.broadcasted_iota(jnp.int32, shape, 1)
    order = order.astype(F32).astype(BF16)
    one, none = jnp.ones((), BF16), jnp.zeros((), BF16)
    parts = []
    for k in range(depth // DEPTH):
        wanted = jnp.broadcast_to(row - float(DEPTH * k), (16, width)).astype(BF16)
        parts.append(jnp.where(order == wanted[None], one, none).reshape(DEPTH, width))
    return jnp.concatenate(parts, axis=0)


def down(row):
    width = row.shape[1]
    order = lax.broadcasted_iota(jnp.int32, (width, DEPTH), 1).astype(F32).astype(BF16)
    column = jnp.broadcast_to(row, (8, width)).T[:, 0:1]
    wanted = jnp.broadcast_to(column, (width, DEPTH)).astype(BF16)
    return jnp.where(order == wanted, jnp.ones((), BF16), jnp.zeros((), BF16))


def spread_out(values, group, groups):
    width = group.shape[1]
    shape = (groups // 16, 16, width)
    order = lax.broadcasted_iota(jnp.int32, shape, 0) * 16 + lax.broadcasted_iota(jnp.int32, shape, 1)
    order = order.astype(F32).astype(BF16)
    hit = order == jnp.broadcast_to(group, (16, width)).astype(BF16)[None]
    parts = []
    for value in values:
        value = jnp.broadcast_to(value, (16, width)).astype(BF16)[None]
        parts.append(jnp.where(hit, value, jnp.zeros((), BF16)).reshape(groups, width))
    return jnp.concatenate(parts, axis=0)


def split_rows(rows):
    length = rows.shape[1]
    high = rows.astype(BF16).astype(F32)
    low = rows - high
    ahead = [pltpu.roll(part, length - 1, 1) for part in (high, low)]
    return jnp.concatenate([high, low] + ahead, axis=0).astype(BF16)


def blend_z(values, fz):
    rows = values.shape[0] // 4
    near = values[:rows] + values[rows : 2 * rows]
    far = values[2 * rows : 3 * rows] + values[3 * rows :]
    return near * (1.0 - fz) + far * fz


def three_parts(values):
    high = values.astype(BF16).astype(F32)
    middle = (values - high).astype(BF16).astype(F32)
    return high, middle, values - high - middle


def three_part_dot(matrix, values):
    high, middle, low = three_parts(matrix)
    second = lambda part: pltpu.roll(part, 64, 1)
    left = jnp.concatenate(
        [high + second(high), middle + second(high), middle + second(low)], axis=1
    )
    a, b, c = three_parts(values)
    blank = jnp.zeros((64 - values.shape[0], values.shape[1]), F32)
    right = []
    for part in (a, b, a, c, b, a):
        right += [part, blank]
    return jnp.dot(
        left.astype(BF16),
        jnp.concatenate(right, axis=0).astype(BF16),
        preferred_element_type=F32,
    )


def tables_kernel(
    cells_z,
    down_ref,
    up_ref,
    scale_ref,
    metric_ref,
    count_ref,
    cell_ref,
    off_ref,
    matrix_ref,
    answer_ref,
    scal_ref,
    slots_ref,
):
    slot = lax.broadcasted_iota(jnp.int32, cell_ref.shape, 1)
    remain = slot - RESIDENT
    heading = remain // CAP
    limit = jnp.where(
        heading <= 0,
        count_ref[0, 0, 0],
        jnp.where(heading == 1, count_ref[0, 0, 1], count_ref[0, 0, 2]),
    )
    sections, rows = down_ref.shape
    cell = cell_ref[...]
    row, place = cell // cells_z, cell % cells_z
    slots_ref[...] = jnp.zeros_like(slots_ref)
    slots_ref[ROW : ROW + 1, :] = row.astype(F32)
    slots_ref[COLUMN : COLUMN + 1, :] = place.astype(F32)
    slots_ref[INNER : INNER + 1, :] = (place % DEPTH).astype(F32)
    slots_ref[GROUP : GROUP + 1, :] = (place // DEPTH * rows + row).astype(F32)
    slots_ref[LIVE : LIVE + 1, :] = jnp.where((remain < 0) | (remain % CAP < limit), 1.0, 0.0)
    slots_ref[EDGE : EDGE + 1, :] = jnp.where(row == rows - 1, off_ref[1:2, :], 0.0)
    lane = lax.broadcasted_iota(jnp.int32, (1, 128), 1)
    at = lambda place: jnp.where(lane == place, 1.0, 0.0)
    matrix_ref[...] = jnp.zeros_like(matrix_ref)
    scal_ref[...] = jnp.zeros_like(scal_ref)
    order = lax.broadcasted_iota(jnp.int32, (rows, 1), 0)
    fy = off_ref[1:2, :]
    weight = jnp.where(order == row, 1.0 - fy, jnp.where(order == row + 1, fy, 0.0))
    edge = slots_ref[EDGE : EDGE + 1, :]
    for k in range(sections):
        lower = []
        row = at(ENTER)
        for i in range(rows):
            row = down_ref[k, i] * row + at(i)
            lower.append(row)
        last = jnp.where(lane < rows, row, 0.0)
        for c in range(COMPS):
            place = COMPS * rows + c
            matrix_ref[k, place : place + 1, :] = pltpu.roll(last, rows * c, 1)
        scal_ref[k, 0:1, :] = row
        row = at(LEAVE)
        for i in reversed(range(rows)):
            row = scale_ref[k, i] * lower[i] + up_ref[k, i] * row
            inner = jnp.where(lane < rows, row, 0.0)
            for c in range(COMPS):
                place = rows * c + i
                matrix_ref[k, place : place + 1, :] = inner if c == 0 else pltpu.roll(inner, rows * c, 1)
            answer_ref[k, i : i + 1, :] = row + metric_ref[i] * at(METRIC)
        if k < sections - 1:
            for i, which, more in ((0, ENTER, 0.0), (1, LEAVE, edge)):
                share = jnp.sum(
                    weight * answer_ref[k, :, which : which + 1], axis=0, keepdims=True
                )
                place = SHARES + 2 * k + i
                slots_ref[place : place + 1, :] = share + more
        scal_ref[k, 1:2, :] = (
            row + scale_ref[k, rows - 1] * at(PIVOT) + up_ref[k, rows - 1] * at(UPWARD)
        )


def two_sides(one_ref, other_ref):
    even = lax.axis_index("gx") % 2 == 0
    one, other = one_ref[...], other_ref[...]
    return jnp.where(even, one, other), jnp.where(even, other, one)


def joined_plane(plane, ef, answer):
    enter, leave = answer[:, ENTER : ENTER + 1], answer[:, LEAVE : LEAVE + 1]
    rows = enter.shape[0]
    return jnp.concatenate(
        [
            plane[rows * c : rows * (c + 1)]
            + enter * ef[c : c + 1]
            + leave * ef[COMPS + c : COMPS + c + 1]
            for c in range(COMPS)
        ],
        axis=0,
    )


def pack(ef_ref, parts):
    for i, part in enumerate(parts):
        ef_ref[6 + i // 2 : 7 + i // 2, CAP * (i % 2) : CAP * (i % 2) + CAP] = part


def unpack(ef):
    return [ef[6 + i // 2 : 7 + i // 2, CAP * (i % 2) : CAP * (i % 2) + CAP] for i in range(4)]


def visitors_kernel(
    number,
    step,
    u_ref,
    ef_ref,
    near_x_ref,
    far_x_ref,
    near_ef_ref,
    far_ef_ref,
    near_old_ref,
    far_old_ref,
    answer_ref,
    out_ref,
):
    cells_z = u_ref.shape[1]
    rows = u_ref.shape[0] // COMPS
    count = COMPS * rows
    _, ef = two_sides(near_ef_ref, far_ef_ref)
    _, old = two_sides(near_old_ref, far_old_ref)
    _, plane = two_sides(near_x_ref, far_x_ref)
    plane = joined_plane(plane, ef, answer_ref[number - 1])
    pad = jnp.zeros((8 - COMPS, cells_z), F32)
    cell, fx, fy, fz = unpack(old)
    *v, tau = unpack(ef)
    row = jnp.floor(cell * (1.0 / cells_z))
    chosen = across(cell - row * cells_z, cells_z)
    behind = split_rows(jnp.concatenate([plane, ef[COMPS : 2 * COMPS], pad], axis=0))
    here = split_rows(jnp.concatenate([u_ref[...], ef_ref[COMPS : 2 * COMPS, :], pad], axis=0))
    blended = blend_z(jnp.dot(behind, chosen, preferred_element_type=F32), fz) * (1.0 - fx)
    blended = blended + blend_z(jnp.dot(here, chosen, preferred_element_type=F32), fz) * fx
    order = lax.broadcasted_iota(jnp.int32, (rows, CAP), 0).astype(F32)
    weight = jnp.where(order == row, 1.0 - fy, jnp.where(order == row + 1.0, fy, 0.0))
    edge = jnp.where(row == rows - 1.0, fy, 0.0)
    for c in range(COMPS):
        part = jnp.sum(blended[rows * c : rows * (c + 1)] * weight, axis=0, keepdims=True)
        fluid = part + blended[count + c : count + c + 1] * edge
        moved = v[c] + step * (tau * (fluid - v[c]))
        out_ref[c : c + 1, :] = jnp.where(cell >= 0.0, moved, 0.0)


def own_plane_kernel(u_ref, slots_ref, off_ref, out_ref, table_ref):
    cells_z = u_ref.shape[1]
    rows = u_ref.shape[0] // COMPS
    table_ref[...] = split_rows(u_ref[...])
    order = lax.broadcasted_iota(jnp.int32, (rows, TILE), 0).astype(F32)
    for t in range(slots_ref.shape[1] // TILE):
        here = slice(t * TILE, (t + 1) * TILE)
        row, column = (slots_ref[d : d + 1, here] for d in (ROW, COLUMN))
        fx, fy, fz = (off_ref[d : d + 1, here] for d in range(3))
        chosen = across(column, cells_z)
        blended = blend_z(jnp.dot(table_ref[...], chosen, preferred_element_type=F32), fz)
        weight = jnp.where(order == row, 1.0 - fy, jnp.where(order == row + 1.0, fy, 0.0))
        weight = weight * (1.0 - fx)
        for c in range(COMPS):
            part = blended[rows * c : rows * (c + 1)] * weight
            out_ref[c : c + 1, here] = jnp.sum(part, axis=0, keepdims=True)


def ahead_plane_kernel(first, one_ref, other_ref, slots_ref, off_ref, own_ref, out_ref, table_ref):
    near_x_ref, far_x_ref = (other_ref, one_ref) if first else (one_ref, other_ref)
    plane, _ = two_sides(near_x_ref, far_x_ref)
    cells_z = plane.shape[1]
    rows = plane.shape[0] // COMPS
    table_ref[...] = split_rows(plane)
    order = lax.broadcasted_iota(jnp.int32, (rows, TILE), 0).astype(F32)
    for t in range(slots_ref.shape[1] // TILE):
        here = slice(t * TILE, (t + 1) * TILE)
        row, column = (slots_ref[d : d + 1, here] for d in (ROW, COLUMN))
        fx, fy, fz = (off_ref[d : d + 1, here] for d in range(3))
        chosen = across(column, cells_z)
        blended = blend_z(jnp.dot(table_ref[...], chosen, preferred_element_type=F32), fz)
        weight = jnp.where(order == row, 1.0 - fy, jnp.where(order == row + 1.0, fy, 0.0)) * fx
        for c in range(COMPS):
            part = blended[rows * c : rows * (c + 1)] * weight
            part = jnp.sum(part, axis=0, keepdims=True)
            out_ref[c : c + 1, here] = own_ref[c : c + 1, here] + part


def section_kernel(number, step, last, *refs):
    first = number == 0
    refs = list(refs)
    take = lambda count: [refs.pop(0) for _ in range(count)]
    u_ref, ym_ref, near_x_ref, far_x_ref, yp_ref, near_ef_ref, far_ef_ref = take(7)
    if first:
        near_x_ref, far_x_ref = far_x_ref, near_x_ref
    slots_ref, off_ref, tau_ref, v_ref, near_ref, matrix_ref, answer_ref, scal_ref = take(8)
    w_ref, pq_ref, v_out_ref = take(3)
    table_ref, spread_ref, chosen_ref = refs

    cells_z = u_ref.shape[1]
    rows = u_ref.shape[0] // COMPS
    count = COMPS * rows
    groups = rows * (cells_z // DEPTH)
    position = lax.axis_index("gy")
    top = jnp.where(position == lax.axis_size("gy") - 1, 0.0, 1.0).astype(F32)
    bottom = jnp.where(position == 0, 0.0, 1.0).astype(F32)
    x_plus, x_minus = two_sides(near_x_ref, far_x_ref)
    ahead, behind = two_sides(near_ef_ref, far_ef_ref)
    if first:
        chip, beside = yp_ref[...], ym_ref[...]
        below = position % 2 == 1
        y_plus = jnp.where(below, beside, chip)[:COMPS] * top
        y_minus = jnp.where(below, chip, beside)[COMPS:] * bottom
        corner = ahead * top
    else:
        y_minus = ym_ref[...] * bottom
        y_plus = yp_ref[COMPS : 2 * COMPS, :]
        corner = ahead[COMPS : 2 * COMPS]
        x_plus, x_minus = (
            joined_plane(plane, ef, answer_ref[number - 1])
            for plane, ef in ((x_plus, ahead), (x_minus, behind))
        )
    if first:
        edge_rows = [
            jnp.concatenate(
                [jnp.zeros((COMPS, cells_z), F32), row, jnp.zeros((2, cells_z), F32)], axis=0
            )
            for row in (y_plus, corner)
        ]
    else:
        edge_rows = [yp_ref[...], ahead]
    table = split_rows(jnp.concatenate(edge_rows, axis=0))
    tall = table.shape[0]
    for k in range(cells_z // DEPTH):
        table_ref[tall * k : tall * (k + 1), :] = table[:, DEPTH * k : DEPTH * (k + 1)]
    upper_half = lax.broadcasted_iota(jnp.int32, (8, TILE), 0) >= COMPS
    for t in range(slots_ref.shape[1] // TILE):
        here = slice(t * TILE, (t + 1) * TILE)
        column, inner, group, live, edge = (
            slots_ref[d : d + 1, here] for d in (COLUMN, INNER, GROUP, LIVE, EDGE)
        )
        fx, fz = off_ref[0:1, here], off_ref[2:3, here]
        chosen_ref[here, :] = down(inner)
        found = jnp.dot(table_ref[...], across(inner, DEPTH), preferred_element_type=F32)
        picked = found[:tall]
        for k in range(1, cells_z // DEPTH):
            picked = jnp.where(column >= float(DEPTH * k), found[tall * k : tall * (k + 1)], picked)
        blended = blend_z(picked, fz)
        if first:
            enters, leaves = 0.0, edge
        else:
            enters, leaves = (
                slots_ref[d : d + 1, here]
                for d in (SHARES + 2 * (number - 1), SHARES + 2 * (number - 1) + 1)
            )
        more = blended[:8] * (1.0 - fx) + blended[8:] * fx
        more = more * jnp.where(upper_half, leaves, enters)
        fluid = near_ref[:, here] + more[:COMPS] + more[COMPS : 2 * COMPS]
        v = v_ref[:, here]
        drag = tau_ref[:, here] * (fluid - v)
        v = v + step * drag
        v_out_ref[:, here] = v * live if last else v
        push = drag * live * (-COUPLING)
        high = push.astype(BF16).astype(F32)
        low = push - high
        pushes = [part[c : c + 1] for part in (high, low) for c in range(COMPS)]
        spread_ref[:, here] = spread_out(pushes, group, groups)
    pushed = jnp.dot(spread_ref[...], chosen_ref[...], preferred_element_type=F32)

    u = u_ref[...]
    slope_x = (x_plus - x_minus) * (0.5 * STREAM_SCALE)
    slope_z = (pltpu.roll(u, cells_z - 1, 1) - pltpu.roll(u, 1, 1)) * (0.5 * SPAN_SCALE)
    metric = 0.5 * answer_ref[number, :, METRIC : METRIC + 1]
    rhs = []
    for c in range(COMPS):
        own = slice(rows * c, rows * (c + 1))
        field = u[own]
        upper = jnp.concatenate([field[1:], y_plus[c : c + 1]], axis=0)
        lower = jnp.concatenate([y_minus[c : c + 1], field[:-1]], axis=0)
        slope_y = (upper - lower) * metric
        convection = -(
            u[:rows] * slope_x[own] + u[rows : 2 * rows] * slope_y + u[2 * rows :] * slope_z[own]
        )
        pieces = []
        for k in range(cells_z // DEPTH):
            high, low = (groups * (c + COMPS * i) + rows * k for i in range(2))
            pieces.append(pushed[high : high + rows] + pushed[low : low + rows])
        force = jnp.concatenate(pieces, axis=1)
        rhs.append(field + step * (convection + force))
    solved = three_part_dot(matrix_ref[number], jnp.concatenate(rhs, axis=0))
    w_ref[...] = solved[:count]
    pq_ref[0:COMPS, :] = solved[count : count + COMPS]
    for c in range(COMPS):
        pq_ref[COMPS + c : COMPS + c + 1, :] = solved[rows * c : rows * c + 1]
    pq_ref[6:, :] = jnp.zeros((pq_ref.shape[0] - 6, cells_z), F32)
    if first:
        for k in range(scal_ref.shape[0]):
            pq_ref[6:8, 128 * k : 128 * (k + 1)] = scal_ref[k]
    if last:
        lower = v_out_ref[:, RESIDENT + CAP : RESIDENT + 2 * CAP]
        upper = v_out_ref[:, RESIDENT + 2 * CAP :]
        even = position % 2 == 0
        for place, part in ((6, jnp.where(even, lower, upper)), (8, jnp.where(even, upper, lower))):
            pq_ref[place : place + 1, 0:CAP] = part[0:1]
            pq_ref[place : place + 1, CAP : 2 * CAP] = part[1:2]
            pq_ref[place + 1 : place + 2, 0:CAP] = part[2:3]


def join_kernel(number, last, blocks, direct, *refs):
    refs = list(refs)
    take = lambda count: [refs.pop(0) for _ in range(count)]
    here = lax.axis_index("gy")
    if direct:
        sources = take(5)
    else:
        (all_ref,) = take(1)
    w_ref, answer_ref = take(2)
    if number > 0:
        (known_ref,) = take(1)
    if last:
        v_ref, from_x_ref, u_ref, moved_ref = take(4)
    else:
        slots_ref, off_ref, tau_ref, v_ref = take(4)
        u_ref, ef_ref, ym_ref = take(3)
        if number == 0:
            (known_ref,) = take(1)
    if direct:
        (all_ref,) = refs
        own_ref, partner_ref, side_ref, other_ref, far_ref = sources
        odd = here % 2 == 1
        all_ref[here] = own_ref[0:8, :]
        all_ref[here ^ 1] = partner_ref[0:8, :]
        near = here ^ jnp.where(odd, 4, 2)
        all_ref[near] = side_ref[0]
        all_ref[near ^ 1] = side_ref[1]
        near = here ^ jnp.where(odd, 2, 4)
        all_ref[near ^ 1] = other_ref[0]
        all_ref[near] = other_ref[1]
        all_ref[here ^ 6] = far_ref[0]
        all_ref[here ^ 7] = far_ref[1]
    rows = w_ref.shape[0] // COMPS
    if number == 0:
        known_ref[...] = all_ref[:, 6:8, 0 : known_ref.shape[2]]

    def scal(k, which, row=1):
        place = 128 * number + which
        return known_ref[k, row : row + 1, place : place + 1]

    zero = jnp.zeros((COMPS, w_ref.shape[1]), F32)
    entering, own_in, at = zero, zero, []
    for k in range(blocks):
        at.append(entering)
        own_in = jnp.where(here == k, entering, own_in)
        entering = all_ref[k, 0:COMPS, :] + scal(k, ENTER, 0) * entering
    leaving, own_out = zero, zero
    for k in reversed(range(blocks)):
        own_out = jnp.where(here == k, leaving, own_out)
        leaving = (
            all_ref[k, COMPS : 2 * COMPS, :] + scal(k, ENTER) * at[k] + scal(k, LEAVE) * leaving
        )
    enter = answer_ref[number, :, ENTER : ENTER + 1]
    leave = answer_ref[number, :, LEAVE : LEAVE + 1]
    for c in range(COMPS):
        own = slice(rows * c, rows * (c + 1))
        u_ref[own, :] = w_ref[own, :] + enter * own_in[c : c + 1] + leave * own_out[c : c + 1]
    below = jnp.maximum(here - 1, 0)
    if last:
        even = here % 2 == 0
        keep_above = jnp.where(here == blocks - 1, 0.0, 1.0).astype(F32)
        keep_below = jnp.where(here == 0, 0.0, 1.0).astype(F32)
        across_chips = jnp.where(even, below, jnp.minimum(here + 1, blocks - 1))
        moved_ref[:, :RESIDENT] = v_ref[:, :RESIDENT]
        moved_ref[:, RESIDENT : RESIDENT + CAP] = from_x_ref[...]
        for c in range(COMPS):
            row, lanes = c // 2, slice(CAP * (c % 2), CAP * (c % 2) + CAP)
            beside = all_ref[across_chips, 6 + row : 7 + row, lanes]
            if direct:
                chip = partner_ref[8 + row : 9 + row, lanes]
            else:
                chip = all_ref[here ^ 1, 8 + row : 9 + row, lanes]
            own = slice(c, c + 1)
            moved_ref[own, RESIDENT + CAP : RESIDENT + 2 * CAP] = (
                jnp.where(even, chip, beside) * keep_above
            )
            moved_ref[own, RESIDENT + 2 * CAP :] = jnp.where(even, beside, chip) * keep_below
    else:
        ef_ref[0:COMPS, :] = own_in
        ef_ref[COMPS : 2 * COMPS, :] = own_out
        leaving = slice(RESIDENT, RESIDENT + CAP)
        if number == 0:
            cell = slots_ref[ROW : ROW + 1, leaving] * float(w_ref.shape[1])
            cell = cell + slots_ref[COLUMN : COLUMN + 1, leaving]
            cell = jnp.where(slots_ref[LIVE : LIVE + 1, leaving] > 0.0, cell, -1.0)
            pack(ef_ref, [cell] + [off_ref[d : d + 1, leaving] for d in range(3)])
        else:
            pack(ef_ref, [v_ref[c : c + 1, leaving] for c in range(COMPS)] + [tau_ref[:, leaving]])
        for c in range(COMPS):
            ym_ref[c : c + 1, :] = (
                scal(below, PIVOT) * own_in[c : c + 1]
                + scal(below, UPWARD) * u_ref[rows * c : rows * c + 1, :]
            )


def on_device(
    velocity,
    y_metric,
    forward_rate,
    backward_rate,
    pivot_inv,
    particle_vel,
    particle_cell,
    particle_offset,
    inverse_tau,
    outgoing_count,
):
    comps, cells_x, cells_y, cells_z = velocity.shape
    assert (comps, cells_x, cells_y) == (COMPS, 1, 16)
    assert cells_z == 2 * CAP and SECTIONS == 3
    slots = particle_vel.shape[1]
    size_x, size_y = lax.axis_size("gx"), lax.axis_size("gy")
    assert size_x % 2 == 0 and size_y % 2 == 0
    diagonal = [
        ((x + 1) % size_x * size_y + (y + 1) % size_y, x * size_y + y)
        for x in range(size_x)
        for y in range(size_y)
    ]
    same_pair = [(i, i ^ 1) for i in range(size_x)]
    next_pair = [(i, (i + (1 if i % 2 else -1)) % size_x) for i in range(size_x)]

    def both_sides(block):
        far = lax.ppermute(block, "gx", next_pair)
        return lax.ppermute(block, "gx", same_pair), far

    next_to = [(i, (i + (1 if i % 2 else -1)) % size_y) for i in range(size_y)]
    flip = lambda bits: [(i, i ^ bits) for i in range(size_y)]
    mixed = [(i, i ^ (4 if i % 2 else 2)) for i in range(size_y)]
    direct = size_y == 8

    u = velocity.reshape(COMPS * cells_y, cells_z)
    first = velocity[:, 0, 0, :]
    final = velocity[:, 0, cells_y - 1, :]
    planes = both_sides(u)
    corner = lax.ppermute(first, ("gx", "gy"), diagonal)
    both = jnp.concatenate([first, final], axis=0)
    ym = lax.ppermute(both, "gy", next_to)
    yp = lax.ppermute(both, "gy", flip(1))
    edges = (corner, corner)

    cell = particle_cell.reshape(1, slots)
    tau = inverse_tau.reshape(1, slots)
    like = lambda *shape: jax.ShapeDtypeStruct(shape, F32)
    matrix, answer, scal, places = call(
        functools.partial(tables_kernel, cells_z),
        (like(SECTIONS, 56, 128), like(SECTIONS, cells_y, 128), like(SECTIONS, 2, 128),
         like(16, slots)),
        scalars(5) + whole_in_vmem(2),
        "tables",
    )(forward_rate, backward_rate, pivot_inv, y_metric, outgoing_count, cell, particle_offset)
    v = particle_vel
    rows = COMPS * cells_y
    field_like, slots_like = like(rows, cells_z), like(COMPS, slots)

    def own_plane(plane):
        return call(
            own_plane_kernel,
            slots_like,
            whole_in_vmem(3),
            "own_plane",
            [pltpu.VMEM((4 * rows, cells_z), BF16)],
        )(plane, places, particle_offset)

    own_near = own_plane(u)
    for k in range(SECTIONS):
        last = k == SECTIONS - 1
        given = planes[::-1] if k == 0 else planes
        near = call(
            functools.partial(ahead_plane_kernel, k == 0),
            slots_like,
            whole_in_vmem(5),
            "ahead_plane",
            [pltpu.VMEM((4 * rows, cells_z), BF16)],
        )(*given, places, particle_offset, own_near)
        sides = (u, ym, *given, yp, *edges)
        out = call(
            functools.partial(section_kernel, k, TIME_STEP * SECTION_WEIGHTS[k], last),
            (field_like, like(16 if last else 8, cells_z), slots_like),
            whole_in_vmem(len(sides) + 8),
            "section",
            [
                pltpu.VMEM((4 * 16 * cells_z // DEPTH, DEPTH), BF16),
                pltpu.VMEM((2 * rows * (cells_z // DEPTH), slots), BF16),
                pltpu.VMEM((slots, DEPTH), BF16),
            ],
        )(*sides, places, particle_offset, tau, v, near, matrix, answer, scal)
        w, pq, v = out[:3]
        if last:
            from_x = call(
                functools.partial(visitors_kernel, k, TIME_STEP * SECTION_WEIGHTS[k]),
                like(COMPS, CAP),
                whole_in_vmem(9),
                "visitors",
            )(u, yp, *planes, *edges, *old_edges, answer)
        if direct:
            partner = lax.ppermute(pq, "gy", flip(1))
            if last:
                partner, from_x = lax.optimization_barrier((partner, from_x))
            pair = jnp.stack([pq[:8], partner[:8]])
            side = lax.ppermute(pair, "gy", mixed)
            far = lax.ppermute(pair, "gy", flip(6))
            other = lax.ppermute(side, "gy", flip(1))
            gathered = (pq, partner, side, other, far)
            scratch = [pltpu.VMEM((size_y, 8, cells_z), F32)]
        else:
            gathered = (lax.all_gather(pq, "gy", axis=0),)
            scratch = []
        if last:
            more, shapes = (v, from_x), (field_like, slots_like)
        else:
            planes = both_sides(w)
            own_near = own_plane(w)
            more = (places, particle_offset, tau, v)
            shapes = (field_like, like(8, cells_z), like(COMPS, cells_z))
        if k == 0:
            shapes = shapes + (like(size_y, 2, 128 * SECTIONS),)
        else:
            more = (known,) + more
        joined = call(
            functools.partial(join_kernel, k, last, size_y, direct),
            shapes,
            whole_in_vmem(len(gathered) + 2 + len(more)),
            "join",
            scratch,
        )(*gathered, w, answer, *more)
        if not last:
            u, yp, ym = joined[:3]
            if k == 0:
                known = joined[3]
            old_edges, edges = edges, both_sides(yp)
    u, moved = joined
    return (u.reshape(velocity.shape), moved)


def solution(mesh):
    return jax.shard_map(
        on_device,
        mesh=mesh,
        in_specs=(
            P(None, "gx", "gy", None),
            P("gy"),
            P(None, "gy"),
            P(None, "gy"),
            P(None, "gy"),
            P(None, ("gx", "gy")),
            P(("gx", "gy")),
            P(None, ("gx", "gy")),
            P(("gx", "gy")),
            P("gx", "gy", None),
        ),
        out_specs=(P(None, "gx", "gy", None), P(None, ("gx", "gy"))),
        check_vma=False,
    )
```
